128 devices in a mesh: grp: 2 (over y_lo), seq: 16 (over z, y_hi, core), tp: 4 (over x).
Axes of the slice: x: 4, y: 4 (y_hi: 2, y_lo: 2; y = y_hi * 2 + y_lo), z: 4, core: 2. Of those that a mesh axis runs over, the one named last changes fastest.
Arguments:
- hidden: bfloat16 [16384, 4096], P(('grp', 'seq'), 'tp'), may hold values from -6 to 6
- neighbours: bfloat16 [512, 128, 896], P(('grp', 'seq'), 'tp'), may hold values from -6 to 6
- block_map: int32 [256, 2], replicated, may hold values from 0 to 511, as said below
- enc_key_weight: bfloat16 [4096, 896], P(None, 'tp'), may hold values from -1 to 1
- enc_value_weight: bfloat16 [4096, 896], P(None, 'tp'), may hold values from -0.09375 to 0.09375
- enc_query_weight: bfloat16 [896, 896], replicated, may hold values from -1 to 1
- enc_out_weight: bfloat16 [896, 896], replicated, may hold values from -0.1875 to 0.1875
- query_weight: bfloat16 [4096, 4096], P(None, 'tp'), may hold values from -1 to 1
- key_weight: bfloat16 [896, 4096], P(None, 'tp'), may hold values from -1 to 1
- value_weight: bfloat16 [896, 4096], P(None, 'tp'), may hold values from -0.1875 to 0.1875
- out_weight: bfloat16 [4096, 4096], P('tp', ('grp', 'seq')), may hold values from -0.09375 to 0.09375
- cotangent: bfloat16 [16384, 4096], P(('grp', 'seq'), 'tp'), may hold values from -6 to 6
Outputs:
- layer_output: bfloat16 [16384, 4096], P(('grp', 'seq'), 'tp')
- encoded: bfloat16 [512, 128, 896], P(('grp', 'seq'), 'tp')
- grad_out_weight: float32 [4096, 4096], P('tp', ('grp', 'seq'))
The draws below stay inside these ranges and needn't reach their ends.
Inputs may be any that keep to these rules, and one draw needn't show every extreme that they name: `block_map`: every neighbour is retrieved by exactly one slot of one block. The 16 neighbours retrieved by the blocks of one index of grp+seq are held by 16 different indices, 1 by each, and the 16 neighbours held by one index are retrieved by blocks of as many different indices, 1 by each.
All inputs are finite; a program needn't handle non-finite values.
Results may differ from the reference program's by a relative error of at most 0.034.
Values may be sent and summed in bfloat16 or wider, within the bound.
No kernel may reach another device: no remote copies, remote signals or barrier semaphores. Data moves between devices by JAX's collectives and lax.ppermute only.
A program may use at most 128 MiB of HBM per device.

```python
import math
import jax
import jax.numpy as jnp
from jax import lax

D = 4096
HEADS = 32
HD = 128
DE = 896
HE = 7
BLOCK_LEN = 64
NEIGH_LEN = 128
PICKS = 2
BLOCK_DEV = 8
TOK_DEV = 512
BLOCKS = 256
TOKENS = 16384
NEIGH = 512
N_TP = 4


def shared_normal(key, salt, rows, cols):
    values = jax.random.normal(jax.random.fold_in(key, salt), (rows, cols), jnp.float32)
    return jnp.clip(values, -5.0, 5.0)


def draw_query_weight(key, part):
    return (shared_normal(key, 101, D, D) / math.sqrt(D)).astype(jnp.bfloat16)


def draw_key_weight(key, part):
    return (shared_normal(key, 102, DE, D) / math.sqrt(DE)).astype(jnp.bfloat16)


def draw_enc_key_weight(key, part):
    return (shared_normal(key, 103, D, DE) / math.sqrt(D)).astype(jnp.bfloat16)


def draw_enc_query_weight(key, part):
    return (shared_normal(key, 104, DE, DE) / math.sqrt(DE)).astype(jnp.bfloat16)


def draw_hidden(key, part):
    key = jax.random.fold_in(key, 5)
    drawn = jnp.clip(jax.random.normal(key, (TOKENS, D), jnp.float32), -6.0, 6.0)
    return drawn.astype(jnp.bfloat16)


def draw_neighbours(key, part):
    key = jax.random.fold_in(key, 6)
    drawn = jnp.clip(jax.random.normal(key, (NEIGH, NEIGH_LEN, DE), jnp.float32), -6.0, 6.0)
    return drawn.astype(jnp.bfloat16)


def draw_block_map(key, part):
    key = jax.random.fold_in(key, 7)
    key_one, key_two, key_three = jax.random.split(key, 3)
    devices = BLOCKS // BLOCK_DEV
    local_count = PICKS * BLOCK_DEV
    placement = jax.random.permutation(key_one, devices).astype(jnp.int32)
    shifts = jax.random.permutation(key_two, devices).astype(jnp.int32)
    scores = jax.random.randint(key_three, (devices, local_count), 0, 2 ** 20, dtype=jnp.int32) * local_count + jnp.arange(local_count, dtype=jnp.int32)[None, :]
    orders = jnp.argsort(scores, axis=1).astype(jnp.int32)
    entries = jnp.arange(local_count, dtype=jnp.int32)
    receiver = jnp.arange(devices, dtype=jnp.int32)[:, None]
    source = placement[(receiver + shifts[entries % devices][None, :]) % devices]
    slot_index = orders[source, entries[None, :]]
    return (source * local_count + slot_index).reshape(BLOCKS, PICKS).astype(jnp.int32)


def raised(values, key, source, target, blocks, factor):
    def block_of(axis_at):
        return (jnp.arange(values.shape[axis_at]) // (values.shape[axis_at] // blocks)).reshape((-1,) + (1,) * (values.ndim - 1 - axis_at))

    one_side = jax.random.permutation(key, blocks)[block_of(target)]
    other_side = (block_of(target) + blocks // 2) % blocks
    return jnp.where((block_of(source) == one_side) | (block_of(source) == other_side), factor * values, values)


def block_scale(own_key, dims, cuts, least, largest):
    def one(dim, parts):
        steps = jax.random.uniform(jax.random.fold_in(jax.random.fold_in(own_key, 6), dim), (parts,), jnp.float32, least / len(cuts), largest / len(cuts))
        return jnp.repeat(jnp.exp(steps), dims[dim] // parts).reshape((-1,) + (1,) * (len(dims) - dim - 1))

    gain = one(*cuts[0])
    for cut in cuts[1:]:
        gain = gain * one(*cut)
    return gain


def noise(own_key, dims, width, most, shards=(), held_as=jnp.bfloat16):
    drawn = jax.random.normal(own_key, dims, jnp.float32) * width
    if len(shards) > 0:
        drawn = block_scale(own_key, dims, shards, -0.22, 0.18) * drawn
    return jnp.clip(drawn, min=-most, max=most).astype(held_as)


def heavy_noise(rng, extent, deviation, bound, cuts, heavy, kind=jnp.bfloat16):
    drawn = deviation * jax.random.normal(rng, extent, jnp.float32)
    if cuts:
        drawn = drawn * block_scale(rng, extent, cuts, -0.22, 0.18)
    return jnp.clip(raised(drawn, jax.random.fold_in(rng, 3), *heavy), -bound, bound).astype(kind)


def setup_inputs(seed: int = 0) -> dict:
    streams_of = jax.random.split(jax.random.key(seed), 13)
    return {
        "hidden": draw_hidden(jax.random.fold_in(streams_of[12], 71), 0),
        "neighbours": draw_neighbours(jax.random.fold_in(streams_of[12], 71), 0),
        "block_map": draw_block_map(jax.random.fold_in(streams_of[12], 71), 0),
        "enc_key_weight": draw_enc_key_weight(jax.random.fold_in(streams_of[12], 71), 0),
        "enc_value_weight": noise(streams_of[4], (D, DE), D ** -0.5, 0.09375, ((1, 4),)),
        "enc_query_weight": draw_enc_query_weight(jax.random.fold_in(streams_of[12], 71), 0),
        "enc_out_weight": noise(streams_of[6], (DE, DE), DE ** -0.5, 0.1875),
        "query_weight": draw_query_weight(jax.random.fold_in(streams_of[12], 71), 0),
        "key_weight": draw_key_weight(jax.random.fold_in(streams_of[12], 71), 0),
        "value_weight": noise(streams_of[9], (DE, D), DE ** -0.5, 0.1875, ((1, 4),)),
        "out_weight": noise(streams_of[10], (D, D), D ** -0.5, 0.09375, ((0, 4), (1, 32))),
        "cotangent": heavy_noise(streams_of[11], (TOKENS, D), 1.0, 6.0, ((0, 32), (1, 4)), (0, 1, 32, 2.75)),
    }


def reference(hidden, neighbours, block_map, enc_key_weight, enc_value_weight, enc_query_weight, enc_out_weight, query_weight, key_weight, value_weight, out_weight, cotangent):
    head_width = DE // HE
    enc_keys = jnp.dot(hidden, enc_key_weight, preferred_element_type=jnp.float32).astype(jnp.bfloat16)
    enc_values = jnp.dot(hidden, enc_value_weight, preferred_element_type=jnp.float32).astype(jnp.bfloat16)
    flat_map = block_map.reshape(-1).astype(jnp.int32)
    parent = jnp.zeros((NEIGH,), jnp.int32).at[flat_map].set(jnp.arange(BLOCKS * PICKS, dtype=jnp.int32) // PICKS)
    block_keys = enc_keys.reshape(BLOCKS, BLOCK_LEN, HE, head_width)[parent].astype(jnp.float32)
    block_values = enc_values.reshape(BLOCKS, BLOCK_LEN, HE, head_width)[parent].astype(jnp.float32)
    enc_queries = jnp.dot(neighbours.reshape(NEIGH * NEIGH_LEN, DE), enc_query_weight, preferred_element_type=jnp.float32).astype(jnp.bfloat16)
    enc_queries = enc_queries.reshape(NEIGH, NEIGH_LEN, HE, head_width)
    enc_scores = jnp.einsum('nqhd,nkhd->nhqk', enc_queries.astype(jnp.float32), block_keys) / math.sqrt(head_width)
    enc_weights = jax.nn.softmax(enc_scores, axis=-1).astype(jnp.bfloat16)
    enc_mixed = jnp.einsum('nhqk,nkhd->nqhd', enc_weights.astype(jnp.float32), block_values).astype(jnp.bfloat16)
    enc_mixed = enc_mixed.reshape(NEIGH * NEIGH_LEN, DE)
    projected = jnp.dot(enc_mixed, enc_out_weight, preferred_element_type=jnp.float32).reshape(NEIGH, NEIGH_LEN, DE)
    encoded = (neighbours.astype(jnp.float32) + projected).astype(jnp.bfloat16)
    queries = jnp.dot(hidden, query_weight, preferred_element_type=jnp.float32).astype(jnp.bfloat16)
    flat_encoded = encoded.reshape(NEIGH * NEIGH_LEN, DE)
    keys = jnp.dot(flat_encoded, key_weight, preferred_element_type=jnp.float32).astype(jnp.bfloat16).reshape(NEIGH, NEIGH_LEN, HEADS, HD)
    values = jnp.dot(flat_encoded, value_weight, preferred_element_type=jnp.float32).astype(jnp.bfloat16).reshape(NEIGH, NEIGH_LEN, HEADS, HD)

    def one_block(index):
        block_queries = lax.dynamic_slice_in_dim(queries, index * BLOCK_LEN, BLOCK_LEN, 0).reshape(BLOCK_LEN, HEADS, HD).astype(jnp.float32)
        picked = lax.dynamic_index_in_dim(block_map, index, 0, keepdims=False).astype(jnp.int32)
        picked_keys = keys[picked].reshape(PICKS * NEIGH_LEN, HEADS, HD).astype(jnp.float32)
        picked_values = values[picked].reshape(PICKS * NEIGH_LEN, HEADS, HD).astype(jnp.float32)
        scores = jnp.einsum('qhd,khd->hqk', block_queries, picked_keys) / math.sqrt(HD)
        weights = jax.nn.softmax(scores, axis=-1).astype(jnp.bfloat16)
        mixed = jnp.einsum('hqk,khd->qhd', weights.astype(jnp.float32), picked_values)
        return mixed.astype(jnp.bfloat16).reshape(BLOCK_LEN, D)
    attended = lax.map(one_block, jnp.arange(BLOCKS, dtype=jnp.int32)).reshape(TOKENS, D)
    group_width = D // N_TP

    def add_group(running, index):
        group_attended = lax.dynamic_slice_in_dim(attended, index * group_width, group_width, 1)
        group_weight = lax.dynamic_slice_in_dim(out_weight, index * group_width, group_width, 0)
        term = jnp.dot(group_attended, group_weight, preferred_element_type=jnp.float32).astype(jnp.bfloat16)
        return (running + lax.optimization_barrier(term).astype(jnp.float32), None)
    summed = lax.scan(add_group, jnp.zeros((TOKENS, D), jnp.float32), jnp.arange(N_TP, dtype=jnp.int32))[0]
    layer_output = (hidden.astype(jnp.float32) + summed).astype(jnp.bfloat16)

    def add_rows(running, index):
        rows_attended = lax.dynamic_slice_in_dim(attended, index * TOK_DEV, TOK_DEV, 0)
        rows_gradient = lax.dynamic_slice_in_dim(cotangent, index * TOK_DEV, TOK_DEV, 0)
        term = lax.dot_general(rows_attended, rows_gradient, (((0,), (0,)), ((), ())), preferred_element_type=jnp.float32).astype(jnp.bfloat16)
        return (running + lax.optimization_barrier(term).astype(jnp.float32), None)
    grad_out_weight = lax.scan(add_rows, jnp.zeros((D, D), jnp.float32), jnp.arange(TOKENS // TOK_DEV, dtype=jnp.int32))[0]
    return (layer_output, encoded, grad_out_weight)
```

```python
import math

import jax
import jax.numpy as jnp
from jax import lax
from jax.experimental import pallas as pl
from jax.experimental.pallas import tpu as pltpu
from jax.sharding import Mesh, PartitionSpec as P

HD = 128
HE = 7
BLOCK_LEN = 64
PICKS = 2
AXES = ("grp", "z", "yhi", "core", "tp")
YZC = ("grp", "z", "yhi", "core")
YZ = ("grp", "z", "yhi")
VMEM_LIMIT = 48 << 20
NEG = -1e30
NT = (((1,), (1,)), ((), ()))
F32 = jnp.float32
BF16 = jnp.bfloat16


def ring(step):
    return [(i, (i + step) % 4) for i in range(4)]


def forward(x):
    return lax.ppermute(x, "tp", ring(1))


def backward(x):
    return lax.ppermute(x, "tp", ring(-1))


def gather_ring(x):
    half = x.shape[0] // 2
    left = forward(x)
    right = backward(x)
    far_top = forward(left[:half])
    far_bottom = backward(right[half:])
    return (x, left, right, far_top, far_bottom)


def swap_pairs():
    def index(g, z, y, c, t):
        return (((g * 4 + z) * 2 + y) * 2 + c) * 4 + t

    pairs = []
    for g in range(2):
        for z in range(4):
            for y in range(2):
                for c in range(2):
                    for t in range(4):
                        pairs.append(
                            (index(g, z, y, c, t), index(t // 2, 2 * (t % 2) + z % 2, y, c, g * 2 + z // 2))
                        )
    return pairs


def assemble(pieces, me):
    own, left, right, far_top, far_bottom = pieces
    rows, width = own.shape
    whole = jnp.zeros((rows, 4 * width), own.dtype)
    whole = lax.dynamic_update_slice(whole, own, (0, me * width))
    whole = lax.dynamic_update_slice(whole, left, (0, (me + 3) % 4 * width))
    whole = lax.dynamic_update_slice(whole, right, (0, (me + 1) % 4 * width))
    whole = lax.dynamic_update_slice(whole, far_top, (0, (me + 2) % 4 * width))
    whole = lax.dynamic_update_slice(whole, far_bottom, (rows // 2, (me + 2) % 4 * width))
    return whole


def encode_kernel(me_ref, q_ref, nb_ref, own_ref, left_ref, right_ref, top_ref, bottom_ref, w_ref, out_ref, k_s, v_s, m_s):
    part = own_ref.shape[0] // 2
    me = me_ref[0]
    for step, ref in ((0, own_ref), (3, left_ref), (1, right_ref)):
        at = pl.ds(pl.multiple_of((me + step) % 4 * part, 32), part)
        k_s[at, :] = ref[:part, :]
        v_s[at, :] = ref[part:, :]
    at = pl.ds(pl.multiple_of((me + 2) % 4 * part, 32), part)
    k_s[at, :] = top_ref[...]
    v_s[at, :] = bottom_ref[...]
    rows, cols = q_ref.shape[0], k_s.shape[1]
    same = (
        lax.broadcasted_iota(jnp.int32, (rows, cols), 0) // BLOCK_LEN
        == lax.broadcasted_iota(jnp.int32, (rows, cols), 1) // BLOCK_LEN
    )
    for h in range(HE):
        at = slice(h * HD, (h + 1) * HD)
        s = jnp.dot(q_ref[:, at], k_s[at, :], preferred_element_type=F32) * (1.0 / math.sqrt(HD))
        s = jnp.where(same, s, NEG)
        p = jnp.exp(s - jnp.max(s, axis=1, keepdims=True))
        p = p / jnp.sum(p, axis=1, keepdims=True)
        m_s[:, at] = lax.dot_general(p.astype(BF16), v_s[at, :], NT, preferred_element_type=F32).astype(BF16)
    out_ref[...] = (
        nb_ref[...].astype(F32) + jnp.dot(m_s[...], w_ref[...], preferred_element_type=F32)
    ).astype(BF16)


def encode(me, queries, neighbours, pieces, weight):
    rows, width = neighbours.shape
    tokens = pieces[0].shape[1]
    vm = pl.BlockSpec(memory_space=pltpu.VMEM)
    return pl.pallas_call(
        encode_kernel,
        out_shape=jax.ShapeDtypeStruct((rows, width), BF16),
        in_specs=[pl.BlockSpec(memory_space=pltpu.SMEM)] + [vm] * 8,
        out_specs=vm,
        scratch_shapes=[
            pltpu.VMEM((width, tokens), BF16),
            pltpu.VMEM((width, tokens), BF16),
            pltpu.VMEM((rows, width), BF16),
        ],
        compiler_params=pltpu.CompilerParams(vmem_limit_bytes=VMEM_LIMIT),
        cost_estimate=pl.CostEstimate(
            flops=2 * rows * width * (width + 2 * tokens), bytes_accessed=4 << 20, transcendentals=HE * rows * tokens
        ),
        name="encode",
    )(me, queries, neighbours, *pieces, weight)


def absorb_kernel(q_ref, w_ref, out_ref):
    blocks = q_ref.shape[0] // BLOCK_LEN
    for h in range(q_ref.shape[1] // HD):
        at = slice(h * HD, (h + 1) * HD)
        res = lax.dot_general(q_ref[:, at], w_ref[:, at], NT, preferred_element_type=F32).astype(BF16)
        for b in range(blocks):
            out_ref[b, h * BLOCK_LEN : (h + 1) * BLOCK_LEN, :] = res[b * BLOCK_LEN : (b + 1) * BLOCK_LEN]


def absorb(queries, weight):
    tokens, width = queries.shape
    depth = weight.shape[0]
    heads = width // HD
    vm = pl.BlockSpec(memory_space=pltpu.VMEM)
    return pl.pallas_call(
        absorb_kernel,
        out_shape=jax.ShapeDtypeStruct((tokens // BLOCK_LEN, heads * BLOCK_LEN, depth), BF16),
        in_specs=[vm] * 2,
        out_specs=vm,
        compiler_params=pltpu.CompilerParams(vmem_limit_bytes=VMEM_LIMIT),
        cost_estimate=pl.CostEstimate(flops=4 * tokens * width * depth, bytes_accessed=6 << 20, transcendentals=0),
        name="absorb",
    )(queries, weight)


def decode_kernel(q_ref, own_ref, left_ref, right_ref, top_ref, bottom_ref, w_ref, out_ref, e_s, m_s):
    blocks = q_ref.shape[0]
    half = blocks // 2
    heads = m_s.shape[0]
    for b in range(blocks):
        at = slice(b * BLOCK_LEN, (b + 1) * BLOCK_LEN)
        far = top_ref if b < half else bottom_ref
        far_at = slice((b % half) * BLOCK_LEN, (b % half + 1) * BLOCK_LEN)
        e_s[b, 0:64, :] = own_ref[at, :]
        e_s[b, 64:128, :] = left_ref[at, :]
        e_s[b, 128:192, :] = right_ref[at, :]
        e_s[b, 192:256, :] = far[far_at, :]
    for b in range(blocks):
        at = slice(b * BLOCK_LEN, (b + 1) * BLOCK_LEN)
        s = lax.dot_general(q_ref[b], e_s[b], NT, preferred_element_type=F32) * (1.0 / math.sqrt(HD))
        p = jnp.exp(s - jnp.max(s, axis=1, keepdims=True))
        p = p / jnp.sum(p, axis=1, keepdims=True)
        mixed = jnp.dot(p.astype(BF16), e_s[b], preferred_element_type=F32).astype(BF16)
        for h in range(heads):
            m_s[h, at, :] = mixed[h * BLOCK_LEN : (h + 1) * BLOCK_LEN]
    for h in range(heads):
        at = slice(h * HD, (h + 1) * HD)
        out_ref[:, at] = jnp.dot(m_s[h], w_ref[:, at], preferred_element_type=F32).astype(BF16)


def decode(queries, pieces, weight):
    blocks, rows, depth = queries.shape
    heads = rows // BLOCK_LEN
    width = weight.shape[1]
    tokens = blocks * BLOCK_LEN
    vm = pl.BlockSpec(memory_space=pltpu.VMEM)
    return pl.pallas_call(
        decode_kernel,
        out_shape=jax.ShapeDtypeStruct((tokens, width), BF16),
        in_specs=[vm] * 7,
        out_specs=vm,
        scratch_shapes=[
            pltpu.VMEM((blocks, 4 * BLOCK_LEN, depth), BF16),
            pltpu.VMEM((heads, tokens, depth), BF16),
        ],
        compiler_params=pltpu.CompilerParams(vmem_limit_bytes=VMEM_LIMIT),
        cost_estimate=pl.CostEstimate(
            flops=2 * tokens * depth * (heads * 512 + 2 * width), bytes_accessed=8 << 20, transcendentals=blocks * rows * 256
        ),
        name="decode",
    )(queries, *pieces, weight)


def per_device(
    hidden,
    neighbours,
    block_map,
    enc_key_weight,
    enc_value_weight,
    enc_query_weight,
    enc_out_weight,
    query_weight,
    key_weight,
    value_weight,
    out_weight,
    cotangent,
):
    me = lax.axis_index("tp")
    me_vec = me.reshape(1).astype(jnp.int32)
    core = lax.axis_index("core")
    self_index = lax.axis_index(YZC)
    devices = 32
    local_count, positions, depth = neighbours.shape
    tok_rows, feat = hidden.shape
    chunks = 2
    chunk = tok_rows // chunks

    flat_map = block_map.reshape(devices, local_count)
    owners = flat_map // local_count
    places = flat_map % local_count
    order = jnp.arange(local_count, dtype=jnp.int32)
    send_place = jnp.sum(jnp.where(owners == self_index, places, 0), axis=1)
    my_owners = lax.dynamic_index_in_dim(owners, self_index, 0, keepdims=False)
    everyone = jnp.arange(devices, dtype=jnp.int32)
    back_slot = jnp.sum(jnp.where(my_owners[None, :] == everyone[:, None], order[None, :], 0), axis=1)
    wanted = self_index * local_count + order
    asker = jnp.sum(
        jnp.where(
            flat_map.reshape(1, -1) == wanted[:, None],
            (jnp.arange(devices * local_count, dtype=jnp.int32) // local_count)[None, :],
            0,
        ),
        axis=1,
    )

    sent = jnp.take(neighbours, send_place, axis=0)
    came = lax.all_to_all(sent, YZC, split_axis=0, concat_axis=0, tiled=True)
    mine = jnp.take(came, my_owners, axis=0).reshape(local_count * positions, depth)

    out_mine = lax.ppermute(out_weight, AXES, swap_pairs())
    out_all = lax.all_gather(out_mine, YZC, axis=0)
    out_all = out_all.reshape(4, 8, feat, HD).transpose(0, 2, 1, 3).reshape(4 * feat, 8 * HD)

    cot = cotangent.T.reshape(4, 2, HD, tok_rows)
    cot_keep = lax.dynamic_index_in_dim(cot, core, 1, keepdims=False).reshape(4 * HD, tok_rows)
    cot_send = lax.dynamic_index_in_dim(cot, 1 - core, 1, keepdims=False).reshape(4 * HD, tok_rows)

    enc_queries = jnp.dot(mine, enc_query_weight, preferred_element_type=F32).astype(BF16)

    wholes = []
    kv_pieces = []
    for i in range(chunks):
        pieces = gather_ring(hidden[i * chunk : (i + 1) * chunk])
        whole = assemble(pieces, me)
        wholes.append(whole)
        key = jnp.dot(whole, enc_key_weight, preferred_element_type=F32).astype(BF16)
        value = jnp.dot(whole, enc_value_weight, preferred_element_type=F32).astype(BF16)
        kv_pieces.append(gather_ring(jnp.concatenate([key.T, value.T], axis=0)))
    absorbed = []
    for i in range(chunks):
        queries = jnp.dot(wholes[i], query_weight, preferred_element_type=F32).astype(BF16)
        absorbed.append(absorb(queries, key_weight))

    span = mine.shape[0] // chunks
    encoded_parts = []
    encoded_pieces = []
    for i in range(chunks):
        at = slice(i * span, (i + 1) * span)
        part = encode(me_vec, enc_queries[at], mine[at], kv_pieces[i], enc_out_weight)
        encoded_parts.append(part)
        encoded_pieces.append(gather_ring(part))

    attended_parts = []
    for i in range(chunks):
        part = decode(absorbed[i], encoded_pieces[i], value_weight)
        attended_parts.append(assemble(gather_ring(part), me))

    encoded_mine = jnp.concatenate(encoded_parts, axis=0).reshape(local_count, positions, depth)
    back = lax.all_to_all(jnp.take(encoded_mine, back_slot, axis=0), YZC, split_axis=0, concat_axis=0, tiled=True)
    encoded = jnp.take(back, asker, axis=0)

    attended = jnp.concatenate(attended_parts, axis=0)

    def product(rows):
        res = jnp.dot(rows, attended, preferred_element_type=F32).astype(BF16)
        return res.reshape(4, HD, 4, feat).transpose(2, 0, 1, 3).reshape(16, HD, feat)

    other = lax.ppermute(product(cot_send), "core", [(0, 1), (1, 0)])
    pair = (product(cot_keep).astype(F32) + other.astype(F32)).astype(BF16)
    traded = lax.all_to_all(pair, YZ, split_axis=0, concat_axis=0, tiled=True)
    summed = jnp.sum(traded.astype(F32), axis=0).astype(BF16)
    final = lax.ppermute(summed, AXES, swap_pairs())
    grad = final.astype(F32).T

    projected = jnp.dot(attended, out_all, preferred_element_type=F32)
    layer_output = (hidden.astype(F32) + projected).astype(BF16)
    return (layer_output, encoded, grad)


def solution(mesh):
    fine = Mesh(mesh.devices.reshape(2, 4, 2, 2, 4), AXES)
    placed = (
        P(YZC, "tp"),
        P(YZC, "tp", None),
        P(),
        P(None, "tp"),
        P(None, "tp"),
        P(),
        P(),
        P(None, "tp"),
        P(None, "tp"),
        P(None, "tp"),
        P("tp", YZC),
        P(YZC, "tp"),
    )
    return jax.shard_map(
        per_device,
        mesh=fine,
        in_specs=placed,
        out_specs=(P(YZC, "tp"), P(YZC, "tp", None), P("tp", YZC)),
        check_vma=False,
    )
```

```python
import math

import jax
import jax.numpy as jnp
from jax import lax
from jax.experimental import pallas as pl
from jax.experimental.pallas import tpu as pltpu
from jax.sharding import Mesh, PartitionSpec as P

HD = 128
HE = 7
BLOCK_LEN = 64
PICKS = 2
AXES = ("grp", "z", "yhi", "core", "tp")
YZC = ("grp", "z", "yhi", "core")
YZ = ("grp", "z", "yhi")
VMEM_LIMIT = 48 << 20
NEG = -1e30
NT = (((1,), (1,)), ((), ()))
F32 = jnp.float32
SCALE = math.log2(math.e) / math.sqrt(HD)
BF16 = jnp.bfloat16


def ring(step):
    return [(i, (i + step) % 4) for i in range(4)]


def gather_ring(x, way):
    left = lax.ppermute(x, "tp", ring(1))
    right = lax.ppermute(x, "tp", ring(-1))
    far = lax.ppermute(left if way > 0 else right, "tp", ring(way))
    return (x, left, right, far)


STEPS = (0, 3, 1, 2)


def index_of(g, z, y, c, t):
    return (((g * 4 + z) * 2 + y) * 2 + c) * 4 + t


def places():
    return [
        (g, z, y, c, t) for g in range(2) for z in range(4) for y in range(2) for c in range(2) for t in range(4)
    ]


def swapped(g, z, y, c, t):
    return index_of(t // 2, 2 * (t % 2) + z % 2, y, c, g * 2 + z // 2)


def swap_pairs(dg=0, dz=0, dy=0):
    return [(index_of(g, z, y, c, t), swapped(g ^ dg, (z + dz) % 4, y ^ dy, c, t)) for g, z, y, c, t in places()]


def y_pairs(dg, dy):
    return [(g * 2 + y, (g ^ dg) * 2 + (y ^ dy)) for g in range(2) for y in range(2)]


def whole_vmem():
    return pl.BlockSpec(memory_space=pltpu.VMEM)


def scalars():
    return pl.BlockSpec(memory_space=pltpu.SMEM)


def key_value_kernel(me_ref, own_ref, left_ref, right_ref, far_ref, k_ref, v_ref, out_ref):
    me = me_ref[0]
    width = own_ref.shape[1]
    part = k_ref.shape[1]
    key = value = None
    for step, ref in zip(STEPS, (own_ref, left_ref, right_ref, far_ref)):
        at = pl.ds(pl.multiple_of((me + step) % 4 * width, 128), width)
        k_term = jnp.dot(ref[...], k_ref[at, :], preferred_element_type=F32)
        v_term = jnp.dot(ref[...], v_ref[at, :], preferred_element_type=F32)
        key = k_term if key is None else key + k_term
        value = v_term if value is None else value + v_term
    out_ref[:part, :] = key.T.astype(BF16)
    out_ref[part:, :] = value.T.astype(BF16)


def key_value(me, pieces, key_weight, value_weight):
    rows = pieces[0].shape[0]
    part = key_weight.shape[1]
    return pl.pallas_call(
        key_value_kernel,
        out_shape=jax.ShapeDtypeStruct((2 * part, rows), BF16),
        in_specs=[scalars()] + [whole_vmem()] * 6,
        out_specs=whole_vmem(),
        compiler_params=pltpu.CompilerParams(vmem_limit_bytes=VMEM_LIMIT),
        cost_estimate=pl.CostEstimate(flops=4 * rows * 4096 * part, bytes_accessed=6 << 20, transcendentals=0),
        name="key_value",
    )(me, *pieces, key_weight, value_weight)


def query_kernel(me_ref, *refs):
    piece_refs, (q_ref, k_ref, out_ref) = refs[:8], refs[8:]
    me = me_ref[0]
    width = piece_refs[0].shape[1]
    rows = piece_refs[0].shape[0]
    blocks = rows // BLOCK_LEN
    for i in range(2):
        total = None
        for step, ref in zip(STEPS, piece_refs[4 * i : 4 * i + 4]):
            at = pl.ds(pl.multiple_of((me + step) % 4 * width, 128), width)
            term = jnp.dot(ref[...], q_ref[at, :], preferred_element_type=F32)
            total = term if total is None else total + term
        queries = total.astype(BF16)
        for h in range(q_ref.shape[1] // HD):
            cut = slice(h * HD, (h + 1) * HD)
            res = lax.dot_general(queries[:, cut], k_ref[:, cut], NT, preferred_element_type=F32) * SCALE
            res = res.astype(BF16)
            for b in range(blocks):
                out_ref[i * blocks + b, h * BLOCK_LEN : (h + 1) * BLOCK_LEN, :] = res[b * BLOCK_LEN : (b + 1) * BLOCK_LEN]


def query(me, pieces, query_weight, key_weight):
    rows = pieces[0].shape[0]
    depth = key_weight.shape[0]
    full, width = query_weight.shape
    blocks = 2 * rows // BLOCK_LEN
    heads = width // HD
    group = 2
    return pl.pallas_call(
        query_kernel,
        grid=(heads // group,),
        out_shape=jax.ShapeDtypeStruct((blocks, heads * BLOCK_LEN, depth), BF16),
        in_specs=[scalars()]
        + [pl.BlockSpec(pieces[0].shape, lambda n: (0, 0))] * 8
        + [pl.BlockSpec((full, group * HD), lambda n: (0, n)), pl.BlockSpec((depth, group * HD), lambda n: (0, n))],
        out_specs=pl.BlockSpec((blocks, group * BLOCK_LEN, depth), lambda n: (0, n, 0)),
        compiler_params=pltpu.CompilerParams(vmem_limit_bytes=VMEM_LIMIT),
        cost_estimate=pl.CostEstimate(
            flops=4 * rows * width * (full + depth), bytes_accessed=20 << 20, transcendentals=0
        ),
        name="query",
    )(me, *pieces, query_weight, key_weight)


def project_kernel(me_ref, *refs):
    piece_refs, (w_ref, hidden_ref, out_ref) = refs[:8], refs[8:]
    me = me_ref[0]
    rows = piece_refs[0].shape[0]
    for i in range(2):
        at = slice(i * rows, (i + 1) * rows)
        total = hidden_ref[at, :].astype(F32)
        for step, ref in zip(STEPS, piece_refs[4 * i : 4 * i + 4]):
            who = (me + step) % 4
            weight = jnp.concatenate([w_ref[who, 0], w_ref[who, 1]], axis=1)
            total = total + jnp.dot(ref[...], weight, preferred_element_type=F32)
        out_ref[at, :] = total.astype(BF16)


def project(me, pieces, out_all, hidden):
    tokens, width = hidden.shape
    feat = out_all.shape[2]
    return pl.pallas_call(
        project_kernel,
        grid=(4,),
        out_shape=jax.ShapeDtypeStruct((tokens, width), BF16),
        in_specs=[scalars()]
        + [pl.BlockSpec(pieces[0].shape, lambda n: (0, 0))] * 8
        + [
            pl.BlockSpec((4, 2, feat, HD), lambda n: (0, n, 0, 0)),
            pl.BlockSpec((tokens, 2 * HD), lambda n: (0, n)),
        ],
        out_specs=pl.BlockSpec((tokens, 2 * HD), lambda n: (0, n)),
        compiler_params=pltpu.CompilerParams(vmem_limit_bytes=VMEM_LIMIT),
        cost_estimate=pl.CostEstimate(flops=8 * tokens * feat * width, bytes_accessed=14 << 20, transcendentals=0),
        name="project",
    )(me, *pieces, out_all, hidden)


def product_kernel(me_ref, *refs):
    piece_refs, (cot_ref, out_ref) = refs[:8], refs[8:]
    me = me_ref[0]
    rows = piece_refs[0].shape[0]
    for r, step in enumerate(STEPS):
        who = (me + step) % 4
        res = jnp.dot(cot_ref[:, :rows], piece_refs[r][...], preferred_element_type=F32)
        res = res + jnp.dot(cot_ref[:, rows:], piece_refs[4 + r][...], preferred_element_type=F32)
        res = res.astype(BF16)
        for p in range(4):
            out_ref[who // 2 * 8 + who % 2 * 4 + p] = res[p * HD : (p + 1) * HD]


def product(me, pieces, cot):
    feat = pieces[0].shape[1]
    return pl.pallas_call(
        product_kernel,
        out_shape=jax.ShapeDtypeStruct((16, HD, feat), BF16),
        in_specs=[scalars()] + [whole_vmem()] * 9,
        out_specs=whole_vmem(),
        compiler_params=pltpu.CompilerParams(vmem_limit_bytes=VMEM_LIMIT),
        cost_estimate=pl.CostEstimate(
            flops=2 * cot.shape[0] * cot.shape[1] * 4 * feat, bytes_accessed=9 << 20, transcendentals=0
        ),
        name="product",
    )(me, *pieces, cot)


def pair_kernel(by_z, at_ref, keep_ref, came_ref, *outs):
    z, yg = at_ref[0], at_ref[1]
    for d in range(4):
        if by_z:
            for g in range(2):
                for y in range(2):
                    at = (g * 4 + (z + d) % 4) * 2 + y
                    outs[d][g * 2 + y] = (keep_ref[at].astype(F32) + came_ref[at].astype(F32)).astype(BF16)
        else:
            other = yg ^ d
            for k in range(4):
                at = (other // 2 * 4 + k) * 2 + other % 2
                outs[d][k] = (keep_ref[at].astype(F32) + came_ref[at].astype(F32)).astype(BF16)


def pair_sum(by_z, at, keep, came):
    count, rows, feat = keep.shape
    half = feat // 2
    place = 0 if by_z else 1
    spec = pl.BlockSpec((count, rows, half), lambda n: (0, 0, place))
    return pl.pallas_call(
        lambda *refs: pair_kernel(by_z, *refs),
        grid=(1,),
        out_shape=[jax.ShapeDtypeStruct((4, rows, half), BF16)] * 4,
        in_specs=[scalars(), spec, spec],
        out_specs=[pl.BlockSpec((4, rows, half), lambda n: (0, 0, 0))] * 4,
        compiler_params=pltpu.CompilerParams(vmem_limit_bytes=VMEM_LIMIT),
        cost_estimate=pl.CostEstimate(flops=count * rows * half, bytes_accessed=6 << 20, transcendentals=0),
        name="pair_sum",
    )(at, keep, came)


def stage_kernel(by_z, at_ref, a_ref, b_ref, c_ref, d_ref, *outs):
    z, yg = at_ref[0], at_ref[1]
    for d in range(4):
        k = yg ^ d if by_z else (z + d) % 4
        total = a_ref[k].astype(F32) + b_ref[k].astype(F32) + c_ref[k].astype(F32) + d_ref[k].astype(F32)
        outs[d][...] = total.astype(BF16)


def stage_sum(by_z, at, parts):
    _, rows, half = parts[0].shape
    return pl.pallas_call(
        lambda *refs: stage_kernel(by_z, *refs),
        out_shape=[jax.ShapeDtypeStruct((rows, half), BF16)] * 4,
        in_specs=[scalars()] + [whole_vmem()] * 4,
        out_specs=[whole_vmem()] * 4,
        compiler_params=pltpu.CompilerParams(vmem_limit_bytes=VMEM_LIMIT),
        cost_estimate=pl.CostEstimate(flops=16 * rows * half, bytes_accessed=3 << 20, transcendentals=0),
        name="stage_sum",
    )(at, *parts)


def last_kernel(*refs):
    out_ref = refs[8]
    half = refs[0].shape[1]
    for i in range(2):
        total = refs[4 * i][...].astype(F32)
        for ref in refs[4 * i + 1 : 4 * i + 4]:
            total = total + ref[...].astype(F32)
        out_ref[i * half : (i + 1) * half, :] = total.T


def last_sum(parts):
    rows, half = parts[0].shape
    return pl.pallas_call(
        last_kernel,
        out_shape=jax.ShapeDtypeStruct((2 * half, rows), F32),
        in_specs=[whole_vmem()] * 8,
        out_specs=whole_vmem(),
        compiler_params=pltpu.CompilerParams(vmem_limit_bytes=VMEM_LIMIT),
        cost_estimate=pl.CostEstimate(flops=8 * rows * half, bytes_accessed=2 << 20, transcendentals=0),
        name="last_sum",
    )(*parts)


def encode_kernel(me_ref, q_ref, nb_ref, own_ref, left_ref, right_ref, far_ref, w_ref, out_ref, k_s, v_s, m_s):
    part = own_ref.shape[0] // 2
    me = me_ref[0]
    for step, ref in zip(STEPS, (own_ref, left_ref, right_ref, far_ref)):
        at = pl.ds(pl.multiple_of((me + step) % 4 * part, 32), part)
        k_s[at, :] = ref[:part, :]
        v_s[at, :] = ref[part:, :]
    rows, cols = q_ref.shape[0], k_s.shape[1]
    same = (
        lax.broadcasted_iota(jnp.int32, (rows, cols), 0) // BLOCK_LEN
        == lax.broadcasted_iota(jnp.int32, (rows, cols), 1) // BLOCK_LEN
    )
    for h in range(HE):
        at = slice(h * HD, (h + 1) * HD)
        s = jnp.dot(q_ref[:, at], k_s[at, :], preferred_element_type=F32) * SCALE
        s = jnp.where(same, s, NEG)
        p = jnp.exp2(s - jnp.max(s, axis=1, keepdims=True))
        p = p * (1.0 / jnp.sum(p, axis=1, keepdims=True))
        m_s[:, at] = lax.dot_general(p.astype(BF16), v_s[at, :], NT, preferred_element_type=F32).astype(BF16)
    out_ref[...] = (
        nb_ref[...].astype(F32) + jnp.dot(m_s[...], w_ref[...], preferred_element_type=F32)
    ).astype(BF16)


def encode(me, queries, neighbours, pieces, weight):
    rows, width = neighbours.shape
    tokens = pieces[0].shape[1]
    vm = pl.BlockSpec(memory_space=pltpu.VMEM)
    return pl.pallas_call(
        encode_kernel,
        out_shape=jax.ShapeDtypeStruct((rows, width), BF16),
        in_specs=[pl.BlockSpec(memory_space=pltpu.SMEM)] + [vm] * 7,
        out_specs=vm,
        scratch_shapes=[
            pltpu.VMEM((width, tokens), BF16),
            pltpu.VMEM((width, tokens), BF16),
            pltpu.VMEM((rows, width), BF16),
        ],
        compiler_params=pltpu.CompilerParams(vmem_limit_bytes=VMEM_LIMIT),
        cost_estimate=pl.CostEstimate(
            flops=2 * rows * width * (width + 2 * tokens), bytes_accessed=4 << 20, transcendentals=HE * rows * tokens
        ),
        name="encode",
    )(me, queries, neighbours, *pieces, weight)


def decode_kernel(q_ref, own_ref, left_ref, right_ref, far_ref, w_ref, out_ref, e_s, m_s):
    blocks = q_ref.shape[0]
    heads = m_s.shape[0]
    for b in range(blocks):
        at = slice(b * BLOCK_LEN, (b + 1) * BLOCK_LEN)
        for k, ref in enumerate((own_ref, left_ref, right_ref, far_ref)):
            e_s[b, k * BLOCK_LEN : (k + 1) * BLOCK_LEN, :] = ref[at, :]
    for b in range(blocks):
        at = slice(b * BLOCK_LEN, (b + 1) * BLOCK_LEN)
        s = lax.dot_general(q_ref[b], e_s[b], NT, preferred_element_type=F32)
        p = jnp.exp2(s - jnp.max(s, axis=1, keepdims=True))
        p = p * (1.0 / jnp.sum(p, axis=1, keepdims=True))
        mixed = jnp.dot(p.astype(BF16), e_s[b], preferred_element_type=F32).astype(BF16)
        for h in range(heads):
            m_s[h, at, :] = mixed[h * BLOCK_LEN : (h + 1) * BLOCK_LEN]
    for h in range(heads):
        at = slice(h * HD, (h + 1) * HD)
        out_ref[:, at] = jnp.dot(m_s[h], w_ref[:, at], preferred_element_type=F32).astype(BF16)


def decode(first, queries, pieces, weight):
    rows, depth = queries.shape[1:]
    heads = rows // BLOCK_LEN
    width = weight.shape[1]
    tokens = pieces[0].shape[0]
    blocks = tokens // BLOCK_LEN
    part = pl.BlockSpec(pieces[0].shape, lambda n: (0, 0))
    return pl.pallas_call(
        decode_kernel,
        grid=(1,),
        out_shape=jax.ShapeDtypeStruct((tokens, width), BF16),
        in_specs=[pl.BlockSpec((blocks, rows, depth), lambda n: (first, 0, 0))]
        + [part] * 4
        + [pl.BlockSpec(weight.shape, lambda n: (0, 0))],
        out_specs=pl.BlockSpec((tokens, width), lambda n: (0, 0)),
        scratch_shapes=[
            pltpu.VMEM((blocks, 4 * BLOCK_LEN, depth), BF16),
            pltpu.VMEM((heads, tokens, depth), BF16),
        ],
        compiler_params=pltpu.CompilerParams(vmem_limit_bytes=VMEM_LIMIT),
        cost_estimate=pl.CostEstimate(
            flops=2 * tokens * depth * (heads * 512 + 2 * width), bytes_accessed=8 << 20, transcendentals=blocks * rows * 256
        ),
        name="decode",
    )(queries, *pieces, weight)


def per_device(
    hidden,
    neighbours,
    block_map,
    enc_key_weight,
    enc_value_weight,
    enc_query_weight,
    enc_out_weight,
    query_weight,
    key_weight,
    value_weight,
    out_weight,
    cotangent,
):
    me = lax.axis_index("tp")
    me_vec = me.reshape(1).astype(jnp.int32)
    core = lax.axis_index("core")
    spot = jnp.stack([lax.axis_index("z"), lax.axis_index("grp") * 2 + lax.axis_index("yhi")]).astype(jnp.int32)
    self_index = lax.axis_index(YZC)
    devices = 32
    local_count, positions, depth = neighbours.shape
    tok_rows, feat = hidden.shape
    chunks = 2
    chunk = tok_rows // chunks

    flat_map = block_map.reshape(devices, local_count)
    owners = flat_map // local_count
    places = flat_map % local_count
    order = jnp.arange(local_count, dtype=jnp.int32)
    send_place = jnp.sum(jnp.where(owners == self_index, places, 0), axis=1)
    my_owners = lax.dynamic_index_in_dim(owners, self_index, 0, keepdims=False)
    everyone = jnp.arange(devices, dtype=jnp.int32)
    back_slot = jnp.sum(jnp.where(my_owners[None, :] == everyone[:, None], order[None, :], 0), axis=1)
    wanted = self_index * local_count + order
    asker = jnp.sum(
        jnp.where(
            flat_map.reshape(1, -1) == wanted[:, None],
            (jnp.arange(devices * local_count, dtype=jnp.int32) // local_count)[None, :],
            0,
        ),
        axis=1,
    )

    def pick(table, index):
        return table.at[index].get(mode="promise_in_bounds")

    came = lax.all_to_all(pick(neighbours, send_place), YZC, split_axis=0, concat_axis=0, tiled=True)
    mine = pick(came, my_owners).reshape(local_count * positions, depth)

    out_mine = lax.ppermute(out_weight, AXES, swap_pairs())
    out_all = lax.all_gather(out_mine, YZC, axis=0).reshape(4, 8, feat, HD)

    cot = cotangent.T.reshape(4, 2, HD, tok_rows)
    cot_keep = lax.dynamic_index_in_dim(cot, core, 1, keepdims=False).reshape(4 * HD, tok_rows)
    cot_send = lax.dynamic_index_in_dim(cot, 1 - core, 1, keepdims=False).reshape(4 * HD, tok_rows)

    enc_queries = jnp.dot(mine, enc_query_weight, preferred_element_type=F32).astype(BF16)

    ways = (1, -1)
    hidden_pieces = [gather_ring(hidden[i * chunk : (i + 1) * chunk], ways[i]) for i in range(chunks)]
    kv_pieces = [
        gather_ring(key_value(me_vec, hidden_pieces[i], enc_key_weight, enc_value_weight), ways[i]) for i in range(chunks)
    ]
    queries = query(me_vec, hidden_pieces[0] + hidden_pieces[1], query_weight, key_weight)

    span = mine.shape[0] // chunks
    encoded_parts = []
    encoded_pieces = []
    for i in range(chunks):
        at = slice(i * span, (i + 1) * span)
        part = encode(me_vec, enc_queries[at], mine[at], kv_pieces[i], enc_out_weight)
        encoded_parts.append(part)
        encoded_pieces.append(gather_ring(part, ways[i]))

    attended = [gather_ring(decode(i, queries, encoded_pieces[i], value_weight), ways[i]) for i in range(chunks)]
    attended = attended[0] + attended[1]

    encoded_mine = jnp.concatenate(encoded_parts, axis=0).reshape(local_count, positions, depth)
    back = lax.all_to_all(pick(encoded_mine, back_slot), YZC, split_axis=0, concat_axis=0, tiled=True)
    encoded = pick(back, asker)

    other = lax.ppermute(product(me_vec, attended, cot_send), "core", [(0, 1), (1, 0)])
    keep = product(me_vec, attended, cot_keep)
    by_z = pair_sum(True, spot, keep, other)
    by_z = [by_z[0]] + [lax.ppermute(by_z[d], "z", ring(d)) for d in (1, 3, 2)]
    by_y = pair_sum(False, spot, keep, other)
    by_y = [by_y[0]] + [lax.ppermute(by_y[d], ("grp", "yhi"), y_pairs(d // 2, d % 2)) for d in (1, 2, 3)]
    last = [
        lax.ppermute(part, AXES, swap_pairs(dg=d // 2, dy=d % 2)) for d, part in enumerate(stage_sum(True, spot, by_z))
    ] + [lax.ppermute(part, AXES, swap_pairs(dz=d)) for d, part in enumerate(stage_sum(False, spot, by_y))]
    layer_output = project(me_vec, attended, out_all, hidden)
    grad = last_sum(last)
    return (layer_output, encoded, grad)


def solution(mesh):
    fine = Mesh(mesh.devices.reshape(2, 4, 2, 2, 4), AXES)
    placed = (
        P(YZC, "tp"),
        P(YZC, "tp", None),
        P(),
        P(None, "tp"),
        P(None, "tp"),
        P(),
        P(),
        P(None, "tp"),
        P(None, "tp"),
        P(None, "tp"),
        P("tp", YZC),
        P(YZC, "tp"),
    )
    return jax.shard_map(
        per_device,
        mesh=fine,
        in_specs=placed,
        out_specs=(P(YZC, "tp"), P(YZC, "tp", None), P("tp", YZC)),
        check_vma=False,
    )
```

```python
import math

import jax
import jax.numpy as jnp
from jax import lax
from jax.experimental import pallas as pl
from jax.experimental.pallas import tpu as pltpu
from jax.sharding import Mesh, PartitionSpec as P

HD = 128
HE = 7
BLOCK_LEN = 64
PICKS = 2
AXES = ("grp", "z", "yhi", "core", "tp")
YZC = ("grp", "z", "yhi", "core")
YZ = ("grp", "z", "yhi")
VMEM_LIMIT = 60 << 20
TAIL_LIMIT = 60 << 20
NEG = -1e30
NT = (((1,), (1,)), ((), ()))
F32 = jnp.float32
SCALE = math.log2(math.e) / math.sqrt(HD)
BF16 = jnp.bfloat16


def ring(step):
    return [(i, (i + step) % 4) for i in range(4)]


def gather_ring(x, way):
    left = lax.ppermute(x, "tp", ring(1))
    right = lax.ppermute(x, "tp", ring(-1))
    far = lax.ppermute(left if way > 0 else right, "tp", ring(way))
    return (x, left, right, far)


def gather_direct(x):
    return (x,) + tuple(lax.ppermute(x, "tp", ring(step)) for step in (1, -1, 2))


STEPS = (0, 3, 1, 2)


def index_of(g, z, y, c, t):
    return (((g * 4 + z) * 2 + y) * 2 + c) * 4 + t


def places():
    return [
        (g, z, y, c, t) for g in range(2) for z in range(4) for y in range(2) for c in range(2) for t in range(4)
    ]


def owner(g, z, y, c, t):
    return index_of(t // 2, 2 * (t % 2) + z % 2, y, c, (t + 2 * g + z // 2) % 4)


def owner_pairs(dg=0, dz=0, dy=0):
    return [(index_of(g, z, y, c, t), owner(g ^ dg, (z + dz) % 4, y ^ dy, c, t)) for g, z, y, c, t in places()]


def source_pairs():
    return [(target, source) for source, target in owner_pairs()]


def y_pairs(dg, dy):
    return [(g * 2 + y, (g ^ dg) * 2 + (y ^ dy)) for g in range(2) for y in range(2)]


def whole_vmem():
    return pl.BlockSpec(memory_space=pltpu.VMEM)


def scalars():
    return pl.BlockSpec(memory_space=pltpu.SMEM)


def anywhere():
    return pl.BlockSpec(memory_space=pl.ANY)


def pick_kernel(tables, index_ref, *refs):
    table_refs, out_ref = refs[:tables], refs[-1]
    size = table_refs[0].shape[0]
    for i in range(out_ref.shape[0]):
        at = index_ref[i]
        if tables == 1:
            out_ref[i] = table_refs[0][at]
        else:
            low = table_refs[0][jnp.minimum(at, size - 1)]
            high = table_refs[1][jnp.maximum(at - size, 0)]
            out_ref[i] = jnp.where(at < size, low, high)


def pick(tables, index, *after):
    shape = index.shape[:1] + tables[0].shape[1:]
    return pl.pallas_call(
        lambda *refs: pick_kernel(len(tables), *refs),
        out_shape=jax.ShapeDtypeStruct(shape, BF16),
        in_specs=[scalars()] + [whole_vmem()] * len(tables) + [anywhere()] * len(after),
        out_specs=whole_vmem(),
        compiler_params=pltpu.CompilerParams(vmem_limit_bytes=VMEM_LIMIT),
        cost_estimate=pl.CostEstimate(flops=0, bytes_accessed=4 * math.prod(shape), transcendentals=0),
        name="pick",
    )(index, *tables, *after)


def rows_kernel(x_ref, *refs):
    refs[-1][...] = x_ref[...]


def rows_of(x, part, *after):
    rows, width = x.shape[0] // 2, x.shape[1]
    return pl.pallas_call(
        rows_kernel,
        grid=(1,),
        out_shape=jax.ShapeDtypeStruct((rows, width), x.dtype),
        in_specs=[pl.BlockSpec((rows, width), lambda n: (part, 0))] + [anywhere()] * len(after),
        out_specs=pl.BlockSpec((rows, width), lambda n: (0, 0)),
        cost_estimate=pl.CostEstimate(flops=0, bytes_accessed=4 * rows * width, transcendentals=0),
        name="rows_of",
    )(x, *after)


def key_value_kernel(me_ref, own_ref, left_ref, right_ref, far_ref, k_ref, v_ref, out_ref):
    me = me_ref[0]
    width = own_ref.shape[1]
    part = k_ref.shape[0]
    for n, w_ref in enumerate((k_ref, v_ref)):
        total = None
        for step, ref in zip(STEPS, (own_ref, left_ref, right_ref, far_ref)):
            at = pl.ds(pl.multiple_of((me + step) % 4 * width, 128), width)
            term = lax.dot_general(w_ref[:, at], ref[...], NT, preferred_element_type=F32)
            total = term if total is None else total + term
        out_ref[n * part : (n + 1) * part, :] = total.astype(BF16)


def key_value(chunk, me, pieces, far, key_weight, value_weight):
    rows, width = far.shape
    part = key_weight.shape[0]

    def whole(shape):
        return pl.BlockSpec(shape, lambda n: (0, 0))

    return pl.pallas_call(
        key_value_kernel,
        grid=(1,),
        out_shape=jax.ShapeDtypeStruct((2 * part, rows), BF16),
        in_specs=[scalars()]
        + [pl.BlockSpec((rows, width), lambda n: (chunk, 0))] * 3
        + [whole(far.shape), whole(key_weight.shape), whole(key_weight.shape)],
        out_specs=whole((2 * part, rows)),
        compiler_params=pltpu.CompilerParams(vmem_limit_bytes=VMEM_LIMIT),
        cost_estimate=pl.CostEstimate(flops=4 * rows * 4096 * part, bytes_accessed=6 << 20, transcendentals=0),
        name="key_value",
    )(me, *pieces, far, key_weight, value_weight)


def query_kernel(me_ref, own_ref, left_ref, right_ref, far_top_ref, far_bottom_ref, w_ref, out_ref, sum_s):
    step = pl.program_id(0)
    half = far_top_ref.shape[0]

    def term(ref):
        return jnp.dot(ref[...], w_ref[...], preferred_element_type=F32)

    @pl.when(step == 0)
    def _():
        sum_s[...] = term(own_ref)

    @pl.when(step == 1)
    def _():
        sum_s[...] += term(left_ref)

    @pl.when(step == 2)
    def _():
        sum_s[...] += term(right_ref)

    @pl.when(step == 3)
    def _():
        out_ref[:half] = (sum_s[:half] + term(far_top_ref)).astype(BF16)
        out_ref[half:] = (sum_s[half:] + term(far_bottom_ref)).astype(BF16)


def step_of(n):
    return (n == 1) * 3 + (n == 2) * 1 + (n == 3) * 2


def query(me, pieces, weight):
    rows, part = pieces[0].shape
    width = weight.shape[1]
    return pl.pallas_call(
        query_kernel,
        grid_spec=pltpu.PrefetchScalarGridSpec(
            num_scalar_prefetch=1,
            grid=(4,),
            in_specs=[pl.BlockSpec(piece.shape, lambda n, me: (0, 0)) for piece in pieces]
            + [pl.BlockSpec((part, width), lambda n, me: ((me[0] + step_of(n)) % 4, 0))],
            out_specs=pl.BlockSpec((rows, width), lambda n, me: (0, 0)),
            scratch_shapes=[pltpu.VMEM((rows, width), F32)],
        ),
        out_shape=jax.ShapeDtypeStruct((rows, width), BF16),
        compiler_params=pltpu.CompilerParams(vmem_limit_bytes=VMEM_LIMIT),
        cost_estimate=pl.CostEstimate(flops=8 * rows * width * part, bytes_accessed=13 << 20, transcendentals=0),
        name="query",
    )(me, *pieces, weight)


def project_kernel(*refs):
    piece_refs, (w_ref, hidden_ref, out_ref) = refs[:8], refs[8:]
    total = hidden_ref[...].astype(F32)
    for r, step in enumerate(STEPS):
        weight = jnp.concatenate([w_ref[step, 0], w_ref[step, 1]], axis=1)
        both = jnp.concatenate([piece_refs[r][...], piece_refs[4 + r][...]], axis=0)
        total = total + jnp.dot(both, weight, preferred_element_type=F32)
    out_ref[...] = total.astype(BF16)


def project(pieces, out_all, hidden):
    tokens, width = hidden.shape
    feat = out_all.shape[2]
    return pl.pallas_call(
        project_kernel,
        grid=(4,),
        out_shape=jax.ShapeDtypeStruct((tokens, width), BF16),
        in_specs=[pl.BlockSpec(pieces[0].shape, lambda n: (0, 0))] * 8
        + [
            pl.BlockSpec((4, 2, feat, HD), lambda n: (0, n, 0, 0)),
            pl.BlockSpec((tokens, 2 * HD), lambda n: (0, n)),
        ],
        out_specs=pl.BlockSpec((tokens, 2 * HD), lambda n: (0, n)),
        compiler_params=pltpu.CompilerParams(vmem_limit_bytes=VMEM_LIMIT),
        cost_estimate=pl.CostEstimate(flops=8 * tokens * feat * width, bytes_accessed=14 << 20, transcendentals=0),
        name="project",
    )(*pieces, out_all, hidden)


def product_kernel(place, spot_ref, *refs):
    piece_refs, cot_ref, store, cot_s = refs[:8], refs[8], refs[9], refs[-1]
    core = spot_ref[place]
    for p in range(4):
        at = pl.ds(pl.multiple_of((2 * p + core) * HD, HD), HD)
        cot_s[p * HD : (p + 1) * HD, :] = cot_ref[:, at].T
    for r, step in enumerate(STEPS):
        both = jnp.concatenate([piece_refs[r][...], piece_refs[4 + r][...]], axis=0)
        res = jnp.dot(cot_s[...], both, preferred_element_type=F32)
        for p in range(4):
            store[step // 2 * 8 + step % 2 * 4 + p] = res[p * HD : (p + 1) * HD].astype(store.dtype)


def keep_kernel(by_z, spot_ref, *refs):
    came_ref, outs, sums = refs[9], refs[10:14], refs[14]
    product_kernel(2, spot_ref, *refs[:9], sums, refs[15])
    z, yg = spot_ref[0], spot_ref[1]
    for d in range(4):
        for k in range(4):
            if by_z:
                at = (k // 2 * 4 + (z + d) % 4) * 2 + k % 2
            else:
                at = ((yg ^ d) // 2 * 4 + k) * 2 + (yg ^ d) % 2
            outs[d][k] = (sums[at] + came_ref[at].astype(F32)).astype(BF16)


def product_call(kernel, name, half, spot, pieces, cot, extra, extra_specs, out_shape, out_specs, scratch):
    feat = pieces[0].shape[1] // 2
    tokens = cot.shape[0]
    cut = pl.BlockSpec((pieces[0].shape[0], feat), lambda n: (0, half))
    return pl.pallas_call(
        kernel,
        grid=(1,),
        out_shape=out_shape,
        in_specs=[scalars()] + [cut] * 8 + [pl.BlockSpec(cot.shape, lambda n: (0, 0))] + extra_specs,
        out_specs=out_specs,
        scratch_shapes=scratch + [pltpu.VMEM((cot.shape[1] // 2, tokens), BF16)],
        compiler_params=pltpu.CompilerParams(vmem_limit_bytes=TAIL_LIMIT),
        cost_estimate=pl.CostEstimate(
            flops=cot.shape[1] * tokens * 4 * feat, bytes_accessed=7 << 20, transcendentals=0
        ),
        name=name,
    )(spot, *pieces, cot, *extra)


def product_send(half, spot, pieces, cot, *after):
    shape = (16, HD, pieces[0].shape[1] // 2)

    def kernel(*refs):
        product_kernel(3, *refs[:10], *refs[10 + len(after) :])

    return product_call(
        kernel,
        "product_send",
        half,
        spot,
        pieces,
        cot,
        after,
        [anywhere()] * len(after),
        jax.ShapeDtypeStruct(shape, BF16),
        pl.BlockSpec(shape, lambda n: (0, 0, 0)),
        [],
    )


def product_keep(by_z, half, spot, pieces, cot, came):
    _, rows, feat = came.shape
    return product_call(
        lambda *refs: keep_kernel(by_z, *refs),
        "product_keep",
        half,
        spot,
        pieces,
        cot,
        (came,),
        [pl.BlockSpec(came.shape, lambda n: (0, 0, 0))],
        [jax.ShapeDtypeStruct((4, rows, feat), BF16)] * 4,
        [pl.BlockSpec((4, rows, feat), lambda n: (0, 0, 0))] * 4,
        [pltpu.VMEM(came.shape, F32)],
    )


def stage_kernel(by_z, at_ref, a_ref, b_ref, c_ref, d_ref, *outs):
    z, yg = at_ref[0], at_ref[1]
    for d in range(4):
        k = yg ^ d if by_z else (z + d) % 4
        total = a_ref[k].astype(F32) + b_ref[k].astype(F32) + c_ref[k].astype(F32) + d_ref[k].astype(F32)
        outs[d][...] = total.astype(BF16)


def stage_sum(by_z, at, parts, *after):
    _, rows, half = parts[0].shape
    step = rows // 2
    return pl.pallas_call(
        lambda *refs: stage_kernel(by_z, *refs[:5], *refs[5 + len(after) :]),
        grid=(2,),
        out_shape=[jax.ShapeDtypeStruct((rows, half), BF16)] * 4,
        in_specs=[scalars()]
        + [pl.BlockSpec((4, step, half), lambda n: (0, n, 0))] * 4
        + [anywhere()] * len(after),
        out_specs=[pl.BlockSpec((step, half), lambda n: (n, 0))] * 4,
        compiler_params=pltpu.CompilerParams(vmem_limit_bytes=TAIL_LIMIT),
        cost_estimate=pl.CostEstimate(flops=16 * rows * half, bytes_accessed=3 << 20, transcendentals=0),
        name="stage_sum",
    )(at, *parts, *after)


def middle_kernel(*refs):
    out_ref = refs[8]
    rows = refs[0].shape[0]
    for i in range(2):
        total = refs[4 * i][...].astype(F32)
        for ref in refs[4 * i + 1 : 4 * i + 4]:
            total = total + ref[...].astype(F32)
        out_ref[i * rows : (i + 1) * rows, :] = total.astype(BF16)


def middle_sum(parts):
    rows, half = parts[0].shape
    return pl.pallas_call(
        middle_kernel,
        out_shape=jax.ShapeDtypeStruct((2 * rows, half), BF16),
        in_specs=[whole_vmem()] * 8,
        out_specs=whole_vmem(),
        cost_estimate=pl.CostEstimate(flops=8 * rows * half, bytes_accessed=2 << 20, transcendentals=0),
        name="middle_sum",
    )(*parts)


def last_kernel(x_ref, out_ref):
    rows, half = x_ref.shape
    for i in range(2):
        cut = slice(i * (rows // 2), (i + 1) * (rows // 2))
        out_ref[i * half : (i + 1) * half, :] = x_ref[cut, :].astype(F32).T


def last_turn(x):
    rows, half = x.shape
    return pl.pallas_call(
        last_kernel,
        out_shape=jax.ShapeDtypeStruct((2 * half, rows // 2), F32),
        in_specs=[whole_vmem()],
        out_specs=whole_vmem(),
        cost_estimate=pl.CostEstimate(flops=rows * half, bytes_accessed=1 << 20, transcendentals=0),
        name="last_turn",
    )(x)


def encode_kernel(me_ref, q_ref, nb_ref, own_ref, left_ref, right_ref, far_ref, w_ref, out_ref, k_s, v_s, m_s):
    part = own_ref.shape[0] // 2
    me = me_ref[0]
    for step, ref in zip(STEPS, (own_ref, left_ref, right_ref, far_ref)):
        at = pl.ds(pl.multiple_of((me + step) % 4 * part, 32), part)
        k_s[at, :] = ref[:part, :]
        v_s[at, :] = ref[part:, :]
    rows, cols = q_ref.shape[0], k_s.shape[1]
    same = (
        lax.broadcasted_iota(jnp.int32, (rows, cols), 0) // BLOCK_LEN
        == lax.broadcasted_iota(jnp.int32, (rows, cols), 1) // BLOCK_LEN
    )
    for h in range(HE):
        at = slice(h * HD, (h + 1) * HD)
        s = jnp.dot(q_ref[:, at], k_s[at, :], preferred_element_type=F32) * SCALE
        s = jnp.where(same, s, NEG)
        p = jnp.exp2(s - jnp.max(s, axis=1, keepdims=True))
        p = p * (1.0 / jnp.sum(p, axis=1, keepdims=True))
        m_s[:, at] = lax.dot_general(p.astype(BF16), v_s[at, :], NT, preferred_element_type=F32).astype(BF16)
    out_ref[...] = (
        nb_ref[...].astype(F32) + jnp.dot(m_s[...], w_ref[...], preferred_element_type=F32)
    ).astype(BF16)


def encode(me, queries, neighbours, pieces, weight):
    rows, width = neighbours.shape
    tokens = pieces[0].shape[1]
    vm = pl.BlockSpec(memory_space=pltpu.VMEM)
    return pl.pallas_call(
        encode_kernel,
        out_shape=jax.ShapeDtypeStruct((rows, width), BF16),
        in_specs=[pl.BlockSpec(memory_space=pltpu.SMEM)] + [vm] * 7,
        out_specs=vm,
        scratch_shapes=[
            pltpu.VMEM((width, tokens), BF16),
            pltpu.VMEM((width, tokens), BF16),
            pltpu.VMEM((rows, width), BF16),
        ],
        compiler_params=pltpu.CompilerParams(vmem_limit_bytes=VMEM_LIMIT),
        cost_estimate=pl.CostEstimate(
            flops=2 * rows * width * (width + 2 * tokens), bytes_accessed=4 << 20, transcendentals=HE * rows * tokens
        ),
        name="encode",
    )(me, queries, neighbours, *pieces, weight)


def decode_kernel(q_ref, own_ref, left_ref, right_ref, far_ref, k_ref, v_ref, out_ref, q_s, m_s):
    heads, tokens, _ = m_s.shape
    blocks = tokens // BLOCK_LEN
    for h in range(heads):
        cut = slice(h * HD, (h + 1) * HD)
        res = lax.dot_general(q_ref[:, cut], k_ref[:, cut], NT, preferred_element_type=F32) * SCALE
        res = res.astype(BF16)
        for b in range(blocks):
            q_s[b, h * BLOCK_LEN : (h + 1) * BLOCK_LEN, :] = res[b * BLOCK_LEN : (b + 1) * BLOCK_LEN]
    for b in range(blocks):
        at = slice(b * BLOCK_LEN, (b + 1) * BLOCK_LEN)
        rows = jnp.concatenate([own_ref[at, :], left_ref[at, :], right_ref[at, :], far_ref[at, :]], axis=0)
        s = lax.dot_general(q_s[b], rows, NT, preferred_element_type=F32)
        p = jnp.exp2(s - jnp.max(s, axis=1, keepdims=True))
        p = p * (1.0 / jnp.sum(p, axis=1, keepdims=True))
        mixed = jnp.dot(p.astype(BF16), rows, preferred_element_type=F32).astype(BF16)
        for h in range(heads):
            m_s[h, at, :] = mixed[h * BLOCK_LEN : (h + 1) * BLOCK_LEN]
    for h in range(heads):
        at = slice(h * HD, (h + 1) * HD)
        out_ref[:, at] = jnp.dot(m_s[h], v_ref[:, at], preferred_element_type=F32).astype(BF16)


def decode(chunk, queries, pieces, key_weight, value_weight):
    tokens, depth = pieces[0].shape
    width = queries.shape[1]
    heads = width // HD
    blocks = tokens // BLOCK_LEN
    rows = heads * BLOCK_LEN

    def whole(shape):
        return pl.BlockSpec(shape, lambda n: (0, 0))

    return pl.pallas_call(
        decode_kernel,
        grid=(1,),
        out_shape=jax.ShapeDtypeStruct((tokens, width), BF16),
        in_specs=[pl.BlockSpec((tokens, width), lambda n: (chunk, 0))]
        + [whole(pieces[0].shape)] * 4
        + [whole(key_weight.shape)] * 2,
        out_specs=whole((tokens, width)),
        scratch_shapes=[pltpu.VMEM((blocks, rows, depth), BF16), pltpu.VMEM((heads, tokens, depth), BF16)],
        compiler_params=pltpu.CompilerParams(vmem_limit_bytes=VMEM_LIMIT),
        cost_estimate=pl.CostEstimate(
            flops=4 * tokens * depth * (heads * 256 + width), bytes_accessed=7 << 20, transcendentals=blocks * rows * 256
        ),
        name="decode",
    )(queries, *pieces, key_weight, value_weight)


def per_device(
    hidden,
    neighbours,
    block_map,
    enc_key_weight,
    enc_value_weight,
    enc_query_weight,
    enc_out_weight,
    query_weight,
    key_weight,
    value_weight,
    out_weight,
    cotangent,
):
    me = lax.axis_index("tp")
    me_vec = me.reshape(1).astype(jnp.int32)
    core = lax.axis_index("core")
    yg = lax.axis_index("grp") * 2 + lax.axis_index("yhi")
    spot = jnp.stack([lax.axis_index("z"), yg, core, 1 - core]).astype(jnp.int32)
    self_index = lax.axis_index(YZC)
    devices = 32
    local_count, positions, depth = neighbours.shape
    tok_rows, feat = hidden.shape
    chunks = 2
    chunk = tok_rows // chunks

    flat_map = block_map.reshape(devices, local_count)
    owners = flat_map // local_count
    places = flat_map % local_count
    order = jnp.arange(local_count, dtype=jnp.int32)
    send_place = jnp.sum(jnp.where(owners == self_index, places, 0), axis=1)
    my_owners = lax.dynamic_index_in_dim(owners, self_index, 0, keepdims=False)
    everyone = jnp.arange(devices, dtype=jnp.int32)
    back_slot = jnp.sum(jnp.where(my_owners[None, :] == everyone[:, None], order[None, :], 0), axis=1)
    wanted = self_index * local_count + order
    asker = jnp.sum(
        jnp.where(
            flat_map.reshape(1, -1) == wanted[:, None],
            (jnp.arange(devices * local_count, dtype=jnp.int32) // local_count)[None, :],
            0,
        ),
        axis=1,
    )

    ways = (1, -1)
    sent = pick([neighbours], send_place)
    left = lax.ppermute(hidden, "tp", ring(1))
    right = lax.ppermute(hidden, "tp", ring(-1))
    fars = [lax.ppermute(rows_of(left, 0, sent), "tp", ring(1)), lax.ppermute(rows_of(right, 1), "tp", ring(-1))]

    came = lax.all_to_all(sent, YZC, split_axis=0, concat_axis=0, tiled=True)
    mine = pick([came], my_owners).reshape(local_count * positions, depth)
    enc_queries = jnp.dot(mine, enc_query_weight, preferred_element_type=F32).astype(BF16)

    kv_pieces = [
        gather_direct(key_value(i, me_vec, (hidden, left, right), fars[i], enc_key_weight.T, enc_value_weight.T))
        for i in range(chunks)
    ]
    queries = query(me_vec, (hidden, left, right, *fars), query_weight)

    same = jnp.zeros((1,), jnp.int32)
    out_mine = lax.ppermute(pick([out_weight[None]], same, left, right), AXES, source_pairs())
    out_all = lax.all_gather(pick([out_mine], same, kv_pieces[0][0])[0], YZC, axis=0).reshape(4, 8, feat, HD)

    span = mine.shape[0] // chunks
    encoded_parts = []
    encoded_pieces = []
    for i in range(chunks):
        at = slice(i * span, (i + 1) * span)
        part = encode(me_vec, enc_queries[at], mine[at], kv_pieces[i], enc_out_weight)
        encoded_parts.append(part.reshape(local_count // chunks, positions, depth))
        encoded_pieces.append(gather_ring(part, ways[i]))

    back = lax.all_to_all(pick(encoded_parts, back_slot), YZC, split_axis=0, concat_axis=0, tiled=True)
    encoded = pick([back], asker)

    own = [decode(i, queries, encoded_pieces[i], key_weight, value_weight) for i in range(chunks)]
    attended = gather_ring(own[0], ways[0]) + gather_ring(own[1], ways[1])
    others = []
    for half in range(2):
        sums = product_send(half, spot, attended, cotangent, encoded)
        others.append(lax.ppermute(sums, "core", [(0, 1), (1, 0)]))
    by_z = product_keep(True, 0, spot, attended, cotangent, others[0])
    by_z = [by_z[0]] + [lax.ppermute(by_z[d], "z", ring(d)) for d in (1, 3, 2)]
    by_y = product_keep(False, 1, spot, attended, cotangent, others[1])
    by_y = [by_y[0]] + [lax.ppermute(by_y[d], ("grp", "yhi"), y_pairs(d // 2, d % 2)) for d in (1, 2, 3)]
    layer_output = project(attended, out_all, hidden)
    to_y = stage_sum(True, spot, by_z, layer_output)
    to_y = [to_y[0]] + [lax.ppermute(to_y[d], ("grp", "yhi"), y_pairs(d // 2, d % 2)) for d in (1, 2, 3)]
    to_z = stage_sum(False, spot, by_y, layer_output)
    to_z = [to_z[0]] + [lax.ppermute(to_z[d], "z", ring(d)) for d in (1, 3, 2)]
    grad = last_turn(lax.ppermute(middle_sum(to_y + to_z), AXES, owner_pairs()))
    return (layer_output, encoded, grad)


def solution(mesh):
    fine = Mesh(mesh.devices.reshape(2, 4, 2, 2, 4), AXES)
    placed = (
        P(YZC, "tp"),
        P(YZC, "tp", None),
        P(),
        P(None, "tp"),
        P(None, "tp"),
        P(),
        P(),
        P(None, "tp"),
        P(None, "tp"),
        P(None, "tp"),
        P("tp", YZC),
        P(YZC, "tp"),
    )
    return jax.shard_map(
        per_device,
        mesh=fine,
        in_specs=placed,
        out_specs=(P(YZC, "tp"), P(YZC, "tp", None), P("tp", YZC)),
        check_vma=False,
    )
```

```python
import math

import jax
import jax.numpy as jnp
from jax import lax
from jax.experimental import pallas as pl
from jax.experimental.pallas import tpu as pltpu
from jax.sharding import Mesh, PartitionSpec as P

HD = 128
HE = 7
BLOCK_LEN = 64
PICKS = 2
AXES = ("grp", "z", "yhi", "core", "tp")
YZC = ("grp", "z", "yhi", "core")
YZ = ("grp", "z", "yhi")
VMEM_LIMIT = 60 << 20
TAIL_LIMIT = 60 << 20
NEG = -1e30
NT = (((1,), (1,)), ((), ()))
F32 = jnp.float32
SCALE = math.log2(math.e) / math.sqrt(HD)
BF16 = jnp.bfloat16


def ring(step):
    return [(i, (i + step) % 4) for i in range(4)]


def gather_ring(x, way):
    left = lax.ppermute(x, "tp", ring(1))
    right = lax.ppermute(x, "tp", ring(-1))
    far = lax.ppermute(left if way > 0 else right, "tp", ring(way))
    return (x, left, right, far)


def gather_direct(x):
    return (x,) + tuple(lax.ppermute(x, "tp", ring(step)) for step in (1, -1, 2))


STEPS = (0, 3, 1, 2)


def index_of(g, z, y, c, t):
    return (((g * 4 + z) * 2 + y) * 2 + c) * 4 + t


def places():
    return [
        (g, z, y, c, t) for g in range(2) for z in range(4) for y in range(2) for c in range(2) for t in range(4)
    ]


def owner(g, z, y, c, t):
    return index_of(t // 2, 2 * (t % 2) + z % 2, y, c, (t + 2 * g + z // 2) % 4)


def owner_pairs(dg=0, dz=0, dy=0):
    return [(index_of(g, z, y, c, t), owner(g ^ dg, (z + dz) % 4, y ^ dy, c, t)) for g, z, y, c, t in places()]


def y_pairs(dg, dy):
    return [(g * 2 + y, (g ^ dg) * 2 + (y ^ dy)) for g in range(2) for y in range(2)]


def whole_vmem():
    return pl.BlockSpec(memory_space=pltpu.VMEM)


def scalars():
    return pl.BlockSpec(memory_space=pltpu.SMEM)


def anywhere():
    return pl.BlockSpec(memory_space=pl.ANY)


def pick_kernel(tables, index_ref, *refs):
    table_refs, out_ref = refs[:tables], refs[-1]
    size = table_refs[0].shape[0]
    for i in range(out_ref.shape[0]):
        at = index_ref[i]
        if tables == 1:
            out_ref[i] = table_refs[0][at]
        else:
            low = table_refs[0][jnp.minimum(at, size - 1)]
            high = table_refs[1][jnp.maximum(at - size, 0)]
            out_ref[i] = jnp.where(at < size, low, high)


def pick(tables, index, *after):
    shape = index.shape[:1] + tables[0].shape[1:]
    return pl.pallas_call(
        lambda *refs: pick_kernel(len(tables), *refs),
        out_shape=jax.ShapeDtypeStruct(shape, BF16),
        in_specs=[scalars()] + [whole_vmem()] * len(tables) + [anywhere()] * len(after),
        out_specs=whole_vmem(),
        compiler_params=pltpu.CompilerParams(vmem_limit_bytes=VMEM_LIMIT),
        cost_estimate=pl.CostEstimate(flops=0, bytes_accessed=4 * math.prod(shape), transcendentals=0),
        name="pick",
    )(index, *tables, *after)


def nothing(*refs):
    pass


def held(x, *after):
    return pl.pallas_call(
        nothing,
        out_shape=jax.ShapeDtypeStruct(x.shape, x.dtype),
        in_specs=[anywhere()] * (1 + len(after)),
        out_specs=anywhere(),
        input_output_aliases={0: 0},
        name="held",
    )(x, *after)


def rows_kernel(x_ref, *refs):
    refs[-1][...] = x_ref[...]


def rows_of(x, part, *after):
    rows, width = x.shape[0] // 2, x.shape[1]
    return pl.pallas_call(
        rows_kernel,
        grid=(1,),
        out_shape=jax.ShapeDtypeStruct((rows, width), x.dtype),
        in_specs=[pl.BlockSpec((rows, width), lambda n: (part, 0))] + [anywhere()] * len(after),
        out_specs=pl.BlockSpec((rows, width), lambda n: (0, 0)),
        cost_estimate=pl.CostEstimate(flops=0, bytes_accessed=4 * rows * width, transcendentals=0),
        name="rows_of",
    )(x, *after)


def key_value_kernel(me_ref, own_ref, left_ref, right_ref, far_ref, k_ref, v_ref, out_ref):
    me = me_ref[0]
    width = own_ref.shape[1]
    part = k_ref.shape[0]
    for n, w_ref in enumerate((k_ref, v_ref)):
        total = None
        for step, ref in zip(STEPS, (own_ref, left_ref, right_ref, far_ref)):
            at = pl.ds(pl.multiple_of((me + step) % 4 * width, 128), width)
            term = lax.dot_general(w_ref[:, at], ref[...], NT, preferred_element_type=F32)
            total = term if total is None else total + term
        out_ref[n * part : (n + 1) * part, :] = total.astype(BF16)


def key_value(chunk, me, pieces, far, key_weight, value_weight):
    rows, width = far.shape
    part = key_weight.shape[0]

    def whole(shape):
        return pl.BlockSpec(shape, lambda n: (0, 0))

    return pl.pallas_call(
        key_value_kernel,
        grid=(1,),
        out_shape=jax.ShapeDtypeStruct((2 * part, rows), BF16),
        in_specs=[scalars()]
        + [pl.BlockSpec((rows, width), lambda n: (chunk, 0))] * 3
        + [whole(far.shape), whole(key_weight.shape), whole(key_weight.shape)],
        out_specs=whole((2 * part, rows)),
        compiler_params=pltpu.CompilerParams(vmem_limit_bytes=VMEM_LIMIT),
        cost_estimate=pl.CostEstimate(flops=4 * rows * 4096 * part, bytes_accessed=6 << 20, transcendentals=0),
        name="key_value",
    )(me, *pieces, far, key_weight, value_weight)


def query_kernel(me_ref, own_ref, left_ref, right_ref, far_top_ref, far_bottom_ref, w_ref, out_ref, sum_s):
    step = pl.program_id(0)
    half = far_top_ref.shape[0]

    def term(ref):
        return jnp.dot(ref[...], w_ref[...], preferred_element_type=F32)

    @pl.when(step == 0)
    def _():
        sum_s[...] = term(own_ref)

    @pl.when(step == 1)
    def _():
        sum_s[...] += term(left_ref)

    @pl.when(step == 2)
    def _():
        sum_s[...] += term(right_ref)

    @pl.when(step == 3)
    def _():
        out_ref[:half] = (sum_s[:half] + term(far_top_ref)).astype(BF16)
        out_ref[half:] = (sum_s[half:] + term(far_bottom_ref)).astype(BF16)


def step_of(n):
    return (n == 1) * 3 + (n == 2) * 1 + (n == 3) * 2


def query(me, pieces, weight):
    rows, part = pieces[0].shape
    width = weight.shape[1]
    return pl.pallas_call(
        query_kernel,
        grid_spec=pltpu.PrefetchScalarGridSpec(
            num_scalar_prefetch=1,
            grid=(4,),
            in_specs=[pl.BlockSpec(piece.shape, lambda n, me: (0, 0)) for piece in pieces]
            + [pl.BlockSpec((part, width), lambda n, me: ((me[0] + step_of(n)) % 4, 0))],
            out_specs=pl.BlockSpec((rows, width), lambda n, me: (0, 0)),
            scratch_shapes=[pltpu.VMEM((rows, width), F32)],
        ),
        out_shape=jax.ShapeDtypeStruct((rows, width), BF16),
        compiler_params=pltpu.CompilerParams(vmem_limit_bytes=VMEM_LIMIT),
        cost_estimate=pl.CostEstimate(flops=8 * rows * width * part, bytes_accessed=13 << 20, transcendentals=0),
        name="query",
    )(me, *pieces, weight)


def project_kernel(top_ref, bottom_ref, w_ref, out_ref):
    attended = jnp.concatenate([top_ref[...], bottom_ref[...]], axis=0)
    for k in range(0, w_ref.shape[0], 2):
        weight = jnp.concatenate([w_ref[k], w_ref[k + 1]], axis=1)
        out_ref[:, k * HD : (k + 2) * HD] = jnp.dot(attended, weight, preferred_element_type=F32).astype(BF16)


def project(top, bottom, out_all, *after):
    rows, feat = top.shape
    count = out_all.shape[0]
    step = 4
    return pl.pallas_call(
        lambda *refs: project_kernel(*refs[:3], refs[-1]),
        grid=(count // step,),
        out_shape=jax.ShapeDtypeStruct((2 * rows, count * HD), BF16),
        in_specs=[pl.BlockSpec(top.shape, lambda n: (0, 0))] * 2
        + [pl.BlockSpec((step, feat, HD), lambda n: (n, 0, 0))]
        + [anywhere()] * len(after),
        out_specs=pl.BlockSpec((2 * rows, step * HD), lambda n: (0, n)),
        compiler_params=pltpu.CompilerParams(vmem_limit_bytes=VMEM_LIMIT),
        cost_estimate=pl.CostEstimate(flops=4 * rows * feat * count * HD, bytes_accessed=14 << 20, transcendentals=0),
        name="project",
    )(top, bottom, out_all, *after)


def product_kernel(place, spot_ref, *refs):
    piece_refs, cot_ref, store, cot_s = refs[:8], refs[8], refs[9], refs[-1]
    core = spot_ref[place]
    for p in range(4):
        at = pl.ds(pl.multiple_of((2 * p + core) * HD, HD), HD)
        cot_s[p * HD : (p + 1) * HD, :] = cot_ref[:, at].T
    for r, step in enumerate(STEPS):
        both = jnp.concatenate([piece_refs[r][...], piece_refs[4 + r][...]], axis=0)
        res = jnp.dot(cot_s[...], both, preferred_element_type=F32)
        for p in range(4):
            store[step // 2 * 8 + step % 2 * 4 + p] = res[p * HD : (p + 1) * HD].astype(store.dtype)


def keep_kernel(by_z, spot_ref, *refs):
    came_ref, outs, (sums, cot_s) = refs[9], refs[-6:-2], refs[-2:]
    product_kernel(2, spot_ref, *refs[:9], sums, cot_s)
    z, yg = spot_ref[0], spot_ref[1]
    for d in range(4):
        for k in range(4):
            if by_z:
                at = (k // 2 * 4 + (z + d) % 4) * 2 + k % 2
            else:
                at = ((yg ^ d) // 2 * 4 + k) * 2 + (yg ^ d) % 2
            outs[d][k] = (sums[at] + came_ref[at].astype(F32)).astype(BF16)


def product_call(kernel, name, half, spot, pieces, cot, extra, extra_specs, out_shape, out_specs, scratch):
    feat = pieces[0].shape[1] // 2
    tokens = cot.shape[0]
    cut = pl.BlockSpec((pieces[0].shape[0], feat), lambda n: (0, half))
    return pl.pallas_call(
        kernel,
        grid=(1,),
        out_shape=out_shape,
        in_specs=[scalars()] + [cut] * 8 + [pl.BlockSpec(cot.shape, lambda n: (0, 0))] + extra_specs,
        out_specs=out_specs,
        scratch_shapes=scratch + [pltpu.VMEM((cot.shape[1] // 2, tokens), BF16)],
        compiler_params=pltpu.CompilerParams(vmem_limit_bytes=TAIL_LIMIT),
        cost_estimate=pl.CostEstimate(
            flops=cot.shape[1] * tokens * 4 * feat, bytes_accessed=7 << 20, transcendentals=0
        ),
        name=name,
    )(spot, *pieces, cot, *extra)


def product_send(half, spot, pieces, cot, *after):
    shape = (16, HD, pieces[0].shape[1] // 2)

    def kernel(*refs):
        product_kernel(3, *refs[:10], *refs[10 + len(after) :])

    return product_call(
        kernel,
        "product_send",
        half,
        spot,
        pieces,
        cot,
        after,
        [anywhere()] * len(after),
        jax.ShapeDtypeStruct(shape, BF16),
        pl.BlockSpec(shape, lambda n: (0, 0, 0)),
        [],
    )


def product_keep(by_z, half, spot, pieces, cot, came, *after):
    _, rows, feat = came.shape
    return product_call(
        lambda *refs: keep_kernel(by_z, *refs),
        "product_keep",
        half,
        spot,
        pieces,
        cot,
        (came, *after),
        [pl.BlockSpec(came.shape, lambda n: (0, 0, 0))] + [anywhere()] * len(after),
        [jax.ShapeDtypeStruct((4, rows, feat), BF16)] * 4,
        [pl.BlockSpec((4, rows, feat), lambda n: (0, 0, 0))] * 4,
        [pltpu.VMEM(came.shape, F32)],
    )


def stage_kernel(by_z, at_ref, a_ref, b_ref, c_ref, d_ref, *outs):
    z, yg = at_ref[0], at_ref[1]
    for d in range(4):
        k = yg ^ d if by_z else (z + d) % 4
        total = a_ref[k].astype(F32) + b_ref[k].astype(F32) + c_ref[k].astype(F32) + d_ref[k].astype(F32)
        outs[d][...] = total.astype(BF16)


def stage_sum(by_z, at, parts, *after):
    _, rows, half = parts[0].shape
    step = rows // 2
    return pl.pallas_call(
        lambda *refs: stage_kernel(by_z, *refs[:5], *refs[5 + len(after) :]),
        grid=(2,),
        out_shape=[jax.ShapeDtypeStruct((rows, half), BF16)] * 4,
        in_specs=[scalars()]
        + [pl.BlockSpec((4, step, half), lambda n: (0, n, 0))] * 4
        + [anywhere()] * len(after),
        out_specs=[pl.BlockSpec((step, half), lambda n: (n, 0))] * 4,
        compiler_params=pltpu.CompilerParams(vmem_limit_bytes=TAIL_LIMIT),
        cost_estimate=pl.CostEstimate(flops=16 * rows * half, bytes_accessed=3 << 20, transcendentals=0),
        name="stage_sum",
    )(at, *parts, *after)


def middle_kernel(*refs):
    out_ref = refs[8]
    rows = refs[0].shape[0]
    for i in range(2):
        total = refs[4 * i][...].astype(F32)
        for ref in refs[4 * i + 1 : 4 * i + 4]:
            total = total + ref[...].astype(F32)
        out_ref[i * rows : (i + 1) * rows, :] = total.astype(BF16)


def middle_sum(parts):
    rows, half = parts[0].shape
    return pl.pallas_call(
        middle_kernel,
        out_shape=jax.ShapeDtypeStruct((2 * rows, half), BF16),
        in_specs=[whole_vmem()] * 8,
        out_specs=whole_vmem(),
        cost_estimate=pl.CostEstimate(flops=8 * rows * half, bytes_accessed=2 << 20, transcendentals=0),
        name="middle_sum",
    )(*parts)


def last_kernel(x_ref, out_ref):
    rows, half = x_ref.shape
    for i in range(2):
        cut = slice(i * (rows // 2), (i + 1) * (rows // 2))
        out_ref[i * half : (i + 1) * half, :] = x_ref[cut, :].astype(F32).T


def last_turn(x):
    rows, half = x.shape
    return pl.pallas_call(
        last_kernel,
        out_shape=jax.ShapeDtypeStruct((2 * half, rows // 2), F32),
        in_specs=[whole_vmem()],
        out_specs=whole_vmem(),
        cost_estimate=pl.CostEstimate(flops=rows * half, bytes_accessed=1 << 20, transcendentals=0),
        name="last_turn",
    )(x)


def encode_kernel(me_ref, q_ref, nb_ref, own_ref, left_ref, right_ref, far_ref, w_ref, out_ref, k_s, v_s, m_s):
    part = own_ref.shape[0] // 2
    me = me_ref[0]
    for step, ref in zip(STEPS, (own_ref, left_ref, right_ref, far_ref)):
        at = pl.ds(pl.multiple_of((me + step) % 4 * part, 32), part)
        k_s[at, :] = ref[:part, :]
        v_s[at, :] = ref[part:, :]
    rows, cols = q_ref.shape[0], k_s.shape[1]
    same = (
        lax.broadcasted_iota(jnp.int32, (rows, cols), 0) // BLOCK_LEN
        == lax.broadcasted_iota(jnp.int32, (rows, cols), 1) // BLOCK_LEN
    )
    for h in range(HE):
        at = slice(h * HD, (h + 1) * HD)
        s = jnp.dot(q_ref[:, at], k_s[at, :], preferred_element_type=F32) * SCALE
        s = jnp.where(same, s, NEG)
        p = jnp.exp2(s - jnp.max(s, axis=1, keepdims=True))
        p = p * (1.0 / jnp.sum(p, axis=1, keepdims=True))
        m_s[:, at] = lax.dot_general(p.astype(BF16), v_s[at, :], NT, preferred_element_type=F32).astype(BF16)
    out_ref[...] = (
        nb_ref[...].astype(F32) + jnp.dot(m_s[...], w_ref[...], preferred_element_type=F32)
    ).astype(BF16)


def encode(chunk, me, queries, neighbours, pieces, weight):
    width = neighbours.shape[1]
    rows = neighbours.shape[0] // 2
    tokens = pieces[0].shape[1]

    def whole(shape):
        return pl.BlockSpec(shape, lambda n: (0, 0))

    part = pl.BlockSpec((rows, width), lambda n: (chunk, 0))
    return pl.pallas_call(
        encode_kernel,
        grid=(1,),
        out_shape=jax.ShapeDtypeStruct((rows, width), BF16),
        in_specs=[scalars(), part, part] + [whole(pieces[0].shape)] * 4 + [whole(weight.shape)],
        out_specs=whole((rows, width)),
        scratch_shapes=[
            pltpu.VMEM((width, tokens), BF16),
            pltpu.VMEM((width, tokens), BF16),
            pltpu.VMEM((rows, width), BF16),
        ],
        compiler_params=pltpu.CompilerParams(vmem_limit_bytes=VMEM_LIMIT),
        cost_estimate=pl.CostEstimate(
            flops=2 * rows * width * (width + 2 * tokens), bytes_accessed=4 << 20, transcendentals=HE * rows * tokens
        ),
        name="encode",
    )(me, queries, neighbours, *pieces, weight)


def decode_kernel(q_ref, own_ref, left_ref, right_ref, far_ref, k_ref, v_ref, out_ref, q_s, m_s):
    heads, tokens, _ = m_s.shape
    blocks = tokens // BLOCK_LEN
    for h in range(heads):
        cut = slice(h * HD, (h + 1) * HD)
        res = lax.dot_general(q_ref[:, cut], k_ref[:, cut], NT, preferred_element_type=F32) * SCALE
        res = res.astype(BF16)
        for b in range(blocks):
            q_s[b, h * BLOCK_LEN : (h + 1) * BLOCK_LEN, :] = res[b * BLOCK_LEN : (b + 1) * BLOCK_LEN]
    for b in range(blocks):
        at = slice(b * BLOCK_LEN, (b + 1) * BLOCK_LEN)
        rows = jnp.concatenate([own_ref[at, :], left_ref[at, :], right_ref[at, :], far_ref[at, :]], axis=0)
        s = lax.dot_general(q_s[b], rows, NT, preferred_element_type=F32)
        p = jnp.exp2(s - jnp.max(s, axis=1, keepdims=True))
        p = p * (1.0 / jnp.sum(p, axis=1, keepdims=True))
        mixed = jnp.dot(p.astype(BF16), rows, preferred_element_type=F32).astype(BF16)
        for h in range(heads):
            m_s[h, at, :] = mixed[h * BLOCK_LEN : (h + 1) * BLOCK_LEN]
    for h in range(heads):
        at = slice(h * HD, (h + 1) * HD)
        out_ref[:, at] = jnp.dot(m_s[h], v_ref[:, at], preferred_element_type=F32).astype(BF16)


def decode(chunk, queries, pieces, key_weight, value_weight):
    tokens, depth = pieces[0].shape
    width = queries.shape[1]
    heads = width // HD
    blocks = tokens // BLOCK_LEN
    rows = heads * BLOCK_LEN

    def whole(shape):
        return pl.BlockSpec(shape, lambda n: (0, 0))

    return pl.pallas_call(
        decode_kernel,
        grid=(1,),
        out_shape=jax.ShapeDtypeStruct((tokens, width), BF16),
        in_specs=[pl.BlockSpec((tokens, width), lambda n: (chunk, 0))]
        + [whole(pieces[0].shape)] * 4
        + [whole(key_weight.shape)] * 2,
        out_specs=whole((tokens, width)),
        scratch_shapes=[pltpu.VMEM((blocks, rows, depth), BF16), pltpu.VMEM((heads, tokens, depth), BF16)],
        compiler_params=pltpu.CompilerParams(vmem_limit_bytes=VMEM_LIMIT),
        cost_estimate=pl.CostEstimate(
            flops=4 * tokens * depth * (heads * 256 + width), bytes_accessed=7 << 20, transcendentals=blocks * rows * 256
        ),
        name="decode",
    )(queries, *pieces, key_weight, value_weight)


def per_device(
    hidden,
    neighbours,
    block_map,
    enc_key_weight,
    enc_value_weight,
    enc_query_weight,
    enc_out_weight,
    query_weight,
    key_weight,
    value_weight,
    out_weight,
    cotangent,
):
    me = lax.axis_index("tp")
    me_vec = me.reshape(1).astype(jnp.int32)
    core = lax.axis_index("core")
    yg = lax.axis_index("grp") * 2 + lax.axis_index("yhi")
    spot = jnp.stack([lax.axis_index("z"), yg, core, 1 - core]).astype(jnp.int32)
    self_index = lax.axis_index(YZC)
    devices = 32
    local_count, positions, depth = neighbours.shape
    tok_rows, feat = hidden.shape
    chunks = 2
    chunk = tok_rows // chunks

    flat_map = block_map.reshape(devices, local_count)
    owners = flat_map // local_count
    places = flat_map % local_count
    order = jnp.arange(local_count, dtype=jnp.int32)
    send_place = jnp.sum(jnp.where(owners == self_index, places, 0), axis=1)
    my_owners = lax.dynamic_index_in_dim(owners, self_index, 0, keepdims=False)
    everyone = jnp.arange(devices, dtype=jnp.int32)
    back_slot = jnp.sum(jnp.where(my_owners[None, :] == everyone[:, None], order[None, :], 0), axis=1)
    wanted = self_index * local_count + order
    asker = jnp.sum(
        jnp.where(
            flat_map.reshape(1, -1) == wanted[:, None],
            (jnp.arange(devices * local_count, dtype=jnp.int32) // local_count)[None, :],
            0,
        ),
        axis=1,
    )

    ways = (1, -1)
    sent = pick([neighbours], send_place)
    left = lax.ppermute(hidden, "tp", ring(1))
    right = lax.ppermute(hidden, "tp", ring(-1))
    fars = [lax.ppermute(rows_of(left, 0, sent), "tp", ring(1)), lax.ppermute(rows_of(right, 1), "tp", ring(-1))]

    came = lax.all_to_all(sent, YZC, split_axis=0, concat_axis=0, tiled=True)
    mine = pick([came], my_owners).reshape(local_count * positions, depth)
    enc_queries = jnp.dot(mine, enc_query_weight, preferred_element_type=F32).astype(BF16)

    kv_pieces = [
        gather_direct(key_value(i, me_vec, (hidden, left, right), fars[i], enc_key_weight.T, enc_value_weight.T))
        for i in range(chunks)
    ]
    queries = query(me_vec, (hidden, left, right, *fars), query_weight)

    out_all = lax.all_gather(out_weight, YZC, axis=0)

    encoded_parts = []
    encoded_pieces = []
    for i in range(chunks):
        part = encode(i, me_vec, enc_queries, mine, kv_pieces[i], enc_out_weight)
        encoded_parts.append(part.reshape(local_count // chunks, positions, depth))
        encoded_pieces.append(gather_ring(part, ways[i]))

    back = lax.all_to_all(pick(encoded_parts, back_slot), YZC, split_axis=0, concat_axis=0, tiled=True)
    encoded = pick([back], asker)

    own = [decode(i, queries, encoded_pieces[i], key_weight, value_weight) for i in range(chunks)]
    attended = gather_ring(own[0], ways[0]) + gather_ring(own[1], ways[1])
    term = project(*own, out_all)

    others = []
    for half in range(2):
        sums = product_send(half, spot, attended, cotangent, encoded if half else term)
        others.append(lax.ppermute(sums, "core", [(0, 1), (1, 0)]))
    by_z = product_keep(True, 0, spot, attended, cotangent, others[0])
    by_z = [by_z[0]] + [lax.ppermute(by_z[d], "z", ring(d)) for d in (1, 3, 2)]
    by_y = product_keep(False, 1, spot, attended, cotangent, others[1])
    by_y = [by_y[0]] + [lax.ppermute(by_y[d], ("grp", "yhi"), y_pairs(d // 2, d % 2)) for d in (1, 2, 3)]
    projected = lax.psum_scatter(held(term, others[0]), "tp", scatter_dimension=1, tiled=True)
    to_y = stage_sum(True, spot, by_z)
    to_y = [to_y[0]] + [lax.ppermute(to_y[d], ("grp", "yhi"), y_pairs(d // 2, d % 2)) for d in (1, 2, 3)]
    to_z = stage_sum(False, spot, by_y)
    to_z = [to_z[0]] + [lax.ppermute(to_z[d], "z", ring(d)) for d in (1, 3, 2)]
    grad = last_turn(lax.ppermute(middle_sum(to_y + to_z), AXES, owner_pairs()))
    layer_output = (hidden.astype(F32) + projected.astype(F32)).astype(BF16)
    return (layer_output, encoded, grad)


def solution(mesh):
    fine = Mesh(mesh.devices.reshape(2, 4, 2, 2, 4), AXES)
    placed = (
        P(YZC, "tp"),
        P(YZC, "tp", None),
        P(),
        P(None, "tp"),
        P(None, "tp"),
        P(),
        P(),
        P(None, "tp"),
        P(None, "tp"),
        P(None, "tp"),
        P("tp", YZC),
        P(YZC, "tp"),
    )
    return jax.shard_map(
        per_device,
        mesh=fine,
        in_specs=placed,
        out_specs=(P(YZC, "tp"), P(YZC, "tp", None), P("tp", YZC)),
        check_vma=False,
    )
```

```python
import math

import jax
import jax.numpy as jnp
from jax import lax
from jax.experimental import pallas as pl
from jax.experimental.pallas import tpu as pltpu
from jax.sharding import Mesh, PartitionSpec as P

HD = 128
HE = 7
BLOCK_LEN = 64
PICKS = 2
AXES = ("grp", "z", "yhi", "core", "tp")
YZC = ("grp", "z", "yhi", "core")
YZ = ("grp", "z", "yhi")
VMEM_LIMIT = 60 << 20
TAIL_LIMIT = 60 << 20
NEG = -1e30
NT = (((1,), (1,)), ((), ()))
F32 = jnp.float32
SCALE = math.log2(math.e) / math.sqrt(HD)
BF16 = jnp.bfloat16


def ring(step):
    return [(i, (i + step) % 4) for i in range(4)]


def gather_ring(x, way):
    left = lax.ppermute(x, "tp", ring(1))
    right = lax.ppermute(x, "tp", ring(-1))
    far = lax.ppermute(left if way > 0 else right, "tp", ring(way))
    return (x, left, right, far)


def gather_direct(x):
    return (x,) + tuple(lax.ppermute(x, "tp", ring(step)) for step in (1, -1, 2))


STEPS = (0, 3, 1, 2)


def index_of(g, z, y, c, t):
    return (((g * 4 + z) * 2 + y) * 2 + c) * 4 + t


def places():
    return [
        (g, z, y, c, t) for g in range(2) for z in range(4) for y in range(2) for c in range(2) for t in range(4)
    ]


def owner(g, z, y, c, t):
    return index_of(t // 2, 2 * (t % 2) + z % 2, y, c, (t + 2 * g + z // 2) % 4)


def owner_pairs(dg=0, dz=0, dy=0):
    return [(index_of(g, z, y, c, t), owner(g ^ dg, (z + dz) % 4, y ^ dy, c, t)) for g, z, y, c, t in places()]


def y_pairs(dg, dy):
    return [(g * 2 + y, (g ^ dg) * 2 + (y ^ dy)) for g in range(2) for y in range(2)]


def whole_vmem():
    return pl.BlockSpec(memory_space=pltpu.VMEM)


def scalars():
    return pl.BlockSpec(memory_space=pltpu.SMEM)


def anywhere():
    return pl.BlockSpec(memory_space=pl.ANY)


def pick_kernel(tables, index_ref, *refs):
    table_refs, out_ref = refs[:tables], refs[-1]
    size = table_refs[0].shape[0]
    for i in range(out_ref.shape[0]):
        at = index_ref[i]
        if tables == 1:
            out_ref[i] = table_refs[0][at]
        else:
            low = table_refs[0][jnp.minimum(at, size - 1)]
            high = table_refs[1][jnp.maximum(at - size, 0)]
            out_ref[i] = jnp.where(at < size, low, high)


def pick(tables, index, *after):
    shape = index.shape[:1] + tables[0].shape[1:]
    return pl.pallas_call(
        lambda *refs: pick_kernel(len(tables), *refs),
        out_shape=jax.ShapeDtypeStruct(shape, BF16),
        in_specs=[scalars()] + [whole_vmem()] * len(tables) + [anywhere()] * len(after),
        out_specs=whole_vmem(),
        compiler_params=pltpu.CompilerParams(vmem_limit_bytes=VMEM_LIMIT),
        cost_estimate=pl.CostEstimate(flops=0, bytes_accessed=4 * math.prod(shape), transcendentals=0),
        name="pick",
    )(index, *tables, *after)


def take_kernel(index_ref, table_ref, w_ref, out_ref, query_ref):
    size = table_ref.shape[1]
    for i in range(index_ref.shape[0]):
        out_ref[i * size : (i + 1) * size, :] = table_ref[index_ref[i]]
    query_ref[...] = jnp.dot(out_ref[...], w_ref[...], preferred_element_type=F32).astype(BF16)


def take_queries(table, index, weight):
    size, width = table.shape[1:]
    rows = index.shape[0] * size
    return pl.pallas_call(
        take_kernel,
        out_shape=[jax.ShapeDtypeStruct((rows, width), BF16)] * 2,
        in_specs=[scalars()] + [whole_vmem()] * 2,
        out_specs=[whole_vmem()] * 2,
        compiler_params=pltpu.CompilerParams(vmem_limit_bytes=VMEM_LIMIT),
        cost_estimate=pl.CostEstimate(flops=2 * rows * width * width, bytes_accessed=6 << 20, transcendentals=0),
        name="take_queries",
    )(index, table, weight)


def nothing(*refs):
    pass


def held(x, *after):
    return pl.pallas_call(
        nothing,
        out_shape=jax.ShapeDtypeStruct(x.shape, x.dtype),
        in_specs=[anywhere()] * (1 + len(after)),
        out_specs=anywhere(),
        input_output_aliases={0: 0},
        name="held",
    )(x, *after)


def rows_kernel(x_ref, *refs):
    refs[-1][...] = x_ref[...]


def rows_of(x, part, *after):
    rows, width = x.shape[0] // 2, x.shape[1]
    return pl.pallas_call(
        rows_kernel,
        grid=(1,),
        out_shape=jax.ShapeDtypeStruct((rows, width), x.dtype),
        in_specs=[pl.BlockSpec((rows, width), lambda n: (part, 0))] + [anywhere()] * len(after),
        out_specs=pl.BlockSpec((rows, width), lambda n: (0, 0)),
        cost_estimate=pl.CostEstimate(flops=0, bytes_accessed=4 * rows * width, transcendentals=0),
        name="rows_of",
    )(x, *after)


def key_value_kernel(me_ref, own_ref, left_ref, right_ref, far_ref, k_ref, v_ref, out_ref):
    me = me_ref[0]
    width = own_ref.shape[1]
    part = k_ref.shape[0]
    for n, w_ref in enumerate((k_ref, v_ref)):
        total = None
        for step, ref in zip(STEPS, (own_ref, left_ref, right_ref, far_ref)):
            at = pl.ds(pl.multiple_of((me + step) % 4 * width, 128), width)
            term = lax.dot_general(w_ref[:, at], ref[...], NT, preferred_element_type=F32)
            total = term if total is None else total + term
        out_ref[n * part : (n + 1) * part, :] = total.astype(BF16)


def key_value(chunk, me, pieces, far, key_weight, value_weight):
    rows, width = far.shape
    part = key_weight.shape[0]

    def whole(shape):
        return pl.BlockSpec(shape, lambda n: (0, 0))

    return pl.pallas_call(
        key_value_kernel,
        grid=(1,),
        out_shape=jax.ShapeDtypeStruct((2 * part, rows), BF16),
        in_specs=[scalars()]
        + [pl.BlockSpec((rows, width), lambda n: (chunk, 0))] * 3
        + [whole(far.shape), whole(key_weight.shape), whole(key_weight.shape)],
        out_specs=whole((2 * part, rows)),
        compiler_params=pltpu.CompilerParams(vmem_limit_bytes=VMEM_LIMIT),
        cost_estimate=pl.CostEstimate(flops=4 * rows * 4096 * part, bytes_accessed=6 << 20, transcendentals=0),
        name="key_value",
    )(me, *pieces, far, key_weight, value_weight)


def query_kernel(me_ref, own_ref, left_ref, right_ref, far_top_ref, far_bottom_ref, w_ref, out_ref, sum_s):
    step = pl.program_id(0)
    half = far_top_ref.shape[0]

    def term(ref):
        return jnp.dot(ref[...], w_ref[...], preferred_element_type=F32)

    @pl.when(step == 0)
    def _():
        sum_s[...] = term(own_ref)

    @pl.when(step == 1)
    def _():
        sum_s[...] += term(left_ref)

    @pl.when(step == 2)
    def _():
        sum_s[...] += term(right_ref)

    @pl.when(step == 3)
    def _():
        out_ref[:half] = (sum_s[:half] + term(far_top_ref)).astype(BF16)
        out_ref[half:] = (sum_s[half:] + term(far_bottom_ref)).astype(BF16)


def step_of(n):
    return (n == 1) * 3 + (n == 2) * 1 + (n == 3) * 2


def query(me, pieces, weight):
    rows, part = pieces[0].shape
    width = weight.shape[1]
    return pl.pallas_call(
        query_kernel,
        grid_spec=pltpu.PrefetchScalarGridSpec(
            num_scalar_prefetch=1,
            grid=(4,),
            in_specs=[pl.BlockSpec(piece.shape, lambda n, me: (0, 0)) for piece in pieces]
            + [pl.BlockSpec((part, width), lambda n, me: ((me[0] + step_of(n)) % 4, 0))],
            out_specs=pl.BlockSpec((rows, width), lambda n, me: (0, 0)),
            scratch_shapes=[pltpu.VMEM((rows, width), F32)],
        ),
        out_shape=jax.ShapeDtypeStruct((rows, width), BF16),
        compiler_params=pltpu.CompilerParams(vmem_limit_bytes=VMEM_LIMIT),
        cost_estimate=pl.CostEstimate(flops=8 * rows * width * part, bytes_accessed=13 << 20, transcendentals=0),
        name="query",
    )(me, *pieces, weight)


def project_kernel(top_ref, bottom_ref, w_ref, out_ref):
    attended = jnp.concatenate([top_ref[...], bottom_ref[...]], axis=0)
    for k in range(0, w_ref.shape[0], 2):
        weight = jnp.concatenate([w_ref[k], w_ref[k + 1]], axis=1)
        out_ref[:, k * HD : (k + 2) * HD] = jnp.dot(attended, weight, preferred_element_type=F32).astype(BF16)


def project(top, bottom, out_all, *after):
    rows, feat = top.shape
    count = out_all.shape[0]
    step = 4
    return pl.pallas_call(
        lambda *refs: project_kernel(*refs[:3], refs[-1]),
        grid=(count // step,),
        out_shape=jax.ShapeDtypeStruct((2 * rows, count * HD), BF16),
        in_specs=[pl.BlockSpec(top.shape, lambda n: (0, 0))] * 2
        + [pl.BlockSpec((step, feat, HD), lambda n: (n, 0, 0))]
        + [anywhere()] * len(after),
        out_specs=pl.BlockSpec((2 * rows, step * HD), lambda n: (0, n)),
        compiler_params=pltpu.CompilerParams(vmem_limit_bytes=VMEM_LIMIT),
        cost_estimate=pl.CostEstimate(flops=4 * rows * feat * count * HD, bytes_accessed=14 << 20, transcendentals=0),
        name="project",
    )(top, bottom, out_all, *after)


def product_kernel(place, spot_ref, *refs):
    piece_refs, cot_ref, store, cot_s = refs[:8], refs[8], refs[9], refs[-1]
    core = spot_ref[place]
    for p in range(4):
        at = pl.ds(pl.multiple_of((2 * p + core) * HD, HD), HD)
        cot_s[p * HD : (p + 1) * HD, :] = cot_ref[:, at].T
    for r, step in enumerate(STEPS):
        both = jnp.concatenate([piece_refs[r][...], piece_refs[4 + r][...]], axis=0)
        res = jnp.dot(cot_s[...], both, preferred_element_type=F32)
        for p in range(4):
            store[step // 2 * 8 + step % 2 * 4 + p] = res[p * HD : (p + 1) * HD].astype(store.dtype)


def keep_kernel(by_z, spot_ref, *refs):
    came_ref, outs, (sums, cot_s) = refs[9], refs[-6:-2], refs[-2:]
    product_kernel(2, spot_ref, *refs[:9], sums, cot_s)
    z, yg = spot_ref[0], spot_ref[1]
    for d in range(4):
        for k in range(4):
            if by_z:
                at = (k // 2 * 4 + (z + d) % 4) * 2 + k % 2
            else:
                at = ((yg ^ d) // 2 * 4 + k) * 2 + (yg ^ d) % 2
            outs[d][k] = (sums[at] + came_ref[at].astype(F32)).astype(BF16)


def product_call(kernel, name, half, spot, pieces, cot, extra, extra_specs, out_shape, out_specs, scratch):
    feat = pieces[0].shape[1] // 2
    tokens = cot.shape[0]
    cut = pl.BlockSpec((pieces[0].shape[0], feat), lambda n: (0, half))
    return pl.pallas_call(
        kernel,
        grid=(1,),
        out_shape=out_shape,
        in_specs=[scalars()] + [cut] * 8 + [pl.BlockSpec(cot.shape, lambda n: (0, 0))] + extra_specs,
        out_specs=out_specs,
        scratch_shapes=scratch + [pltpu.VMEM((cot.shape[1] // 2, tokens), BF16)],
        compiler_params=pltpu.CompilerParams(vmem_limit_bytes=TAIL_LIMIT),
        cost_estimate=pl.CostEstimate(
            flops=cot.shape[1] * tokens * 4 * feat, bytes_accessed=7 << 20, transcendentals=0
        ),
        name=name,
    )(spot, *pieces, cot, *extra)


def product_send(half, spot, pieces, cot, *after):
    shape = (16, HD, pieces[0].shape[1] // 2)

    def kernel(*refs):
        product_kernel(3, *refs[:10], *refs[10 + len(after) :])

    return product_call(
        kernel,
        "product_send",
        half,
        spot,
        pieces,
        cot,
        after,
        [anywhere()] * len(after),
        jax.ShapeDtypeStruct(shape, BF16),
        pl.BlockSpec(shape, lambda n: (0, 0, 0)),
        [],
    )


def product_keep(by_z, half, spot, pieces, cot, came, *after):
    _, rows, feat = came.shape
    return product_call(
        lambda *refs: keep_kernel(by_z, *refs),
        "product_keep",
        half,
        spot,
        pieces,
        cot,
        (came, *after),
        [pl.BlockSpec(came.shape, lambda n: (0, 0, 0))] + [anywhere()] * len(after),
        [jax.ShapeDtypeStruct((4, rows, feat), BF16)] * 4,
        [pl.BlockSpec((4, rows, feat), lambda n: (0, 0, 0))] * 4,
        [pltpu.VMEM(came.shape, F32)],
    )


def stage_kernel(by_z, at_ref, a_ref, b_ref, c_ref, d_ref, *outs):
    z, yg = at_ref[0], at_ref[1]
    for d in range(4):
        k = yg ^ d if by_z else (z + d) % 4
        total = a_ref[k].astype(F32) + b_ref[k].astype(F32) + c_ref[k].astype(F32) + d_ref[k].astype(F32)
        outs[d][...] = total.astype(BF16)


def stage_sum(by_z, at, parts, *after):
    _, rows, half = parts[0].shape
    step = rows // 2
    return pl.pallas_call(
        lambda *refs: stage_kernel(by_z, *refs[:5], *refs[5 + len(after) :]),
        grid=(2,),
        out_shape=[jax.ShapeDtypeStruct((rows, half), BF16)] * 4,
        in_specs=[scalars()]
        + [pl.BlockSpec((4, step, half), lambda n: (0, n, 0))] * 4
        + [anywhere()] * len(after),
        out_specs=[pl.BlockSpec((step, half), lambda n: (n, 0))] * 4,
        compiler_params=pltpu.CompilerParams(vmem_limit_bytes=TAIL_LIMIT),
        cost_estimate=pl.CostEstimate(flops=16 * rows * half, bytes_accessed=3 << 20, transcendentals=0),
        name="stage_sum",
    )(at, *parts, *after)


def middle_kernel(*refs):
    out_ref = refs[8]
    rows = refs[0].shape[0]
    for i in range(2):
        total = refs[4 * i][...].astype(F32)
        for ref in refs[4 * i + 1 : 4 * i + 4]:
            total = total + ref[...].astype(F32)
        out_ref[i * rows : (i + 1) * rows, :] = total.astype(BF16)


def middle_sum(parts):
    rows, half = parts[0].shape
    return pl.pallas_call(
        middle_kernel,
        out_shape=jax.ShapeDtypeStruct((2 * rows, half), BF16),
        in_specs=[whole_vmem()] * 8,
        out_specs=whole_vmem(),
        cost_estimate=pl.CostEstimate(flops=8 * rows * half, bytes_accessed=2 << 20, transcendentals=0),
        name="middle_sum",
    )(*parts)


def last_kernel(x_ref, out_ref):
    rows, half = x_ref.shape
    for i in range(2):
        cut = slice(i * (rows // 2), (i + 1) * (rows // 2))
        out_ref[i * half : (i + 1) * half, :] = x_ref[cut, :].astype(F32).T


def last_turn(x):
    rows, half = x.shape
    return pl.pallas_call(
        last_kernel,
        out_shape=jax.ShapeDtypeStruct((2 * half, rows // 2), F32),
        in_specs=[whole_vmem()],
        out_specs=whole_vmem(),
        cost_estimate=pl.CostEstimate(flops=rows * half, bytes_accessed=1 << 20, transcendentals=0),
        name="last_turn",
    )(x)


def encode_kernel(me_ref, q_ref, nb_ref, own_ref, left_ref, right_ref, far_ref, w_ref, out_ref, k_s, v_s, m_s):
    part = own_ref.shape[0] // 2
    me = me_ref[0]
    for step, ref in zip(STEPS, (own_ref, left_ref, right_ref, far_ref)):
        at = pl.ds(pl.multiple_of((me + step) % 4 * part, 32), part)
        k_s[at, :] = ref[:part, :]
        v_s[at, :] = ref[part:, :]
    rows, cols = q_ref.shape[0], k_s.shape[1]
    same = (
        lax.broadcasted_iota(jnp.int32, (rows, cols), 0) // BLOCK_LEN
        == lax.broadcasted_iota(jnp.int32, (rows, cols), 1) // BLOCK_LEN
    )
    for h in range(HE):
        at = slice(h * HD, (h + 1) * HD)
        s = jnp.dot(q_ref[:, at], k_s[at, :], preferred_element_type=F32) * SCALE
        s = jnp.where(same, s, NEG)
        p = jnp.exp2(s - jnp.max(s, axis=1, keepdims=True))
        p = p * (1.0 / jnp.sum(p, axis=1, keepdims=True))
        m_s[:, at] = lax.dot_general(p.astype(BF16), v_s[at, :], NT, preferred_element_type=F32).astype(BF16)
    out_ref[...] = (
        nb_ref[...].astype(F32) + jnp.dot(m_s[...], w_ref[...], preferred_element_type=F32)
    ).astype(BF16)


def encode(chunk, me, queries, neighbours, pieces, weight):
    width = neighbours.shape[1]
    rows = neighbours.shape[0] // 2
    tokens = pieces[0].shape[1]

    def whole(shape):
        return pl.BlockSpec(shape, lambda n: (0, 0))

    part = pl.BlockSpec((rows, width), lambda n: (chunk, 0))
    return pl.pallas_call(
        encode_kernel,
        grid=(1,),
        out_shape=jax.ShapeDtypeStruct((rows, width), BF16),
        in_specs=[scalars(), part, part] + [whole(pieces[0].shape)] * 4 + [whole(weight.shape)],
        out_specs=whole((rows, width)),
        scratch_shapes=[
            pltpu.VMEM((width, tokens), BF16),
            pltpu.VMEM((width, tokens), BF16),
            pltpu.VMEM((rows, width), BF16),
        ],
        compiler_params=pltpu.CompilerParams(vmem_limit_bytes=VMEM_LIMIT),
        cost_estimate=pl.CostEstimate(
            flops=2 * rows * width * (width + 2 * tokens), bytes_accessed=4 << 20, transcendentals=HE * rows * tokens
        ),
        name="encode",
    )(me, queries, neighbours, *pieces, weight)


def decode_kernel(q_ref, own_ref, left_ref, right_ref, far_ref, k_ref, v_ref, out_ref, q_s, m_s):
    heads, tokens, _ = m_s.shape
    blocks = tokens // BLOCK_LEN
    for h in range(heads):
        cut = slice(h * HD, (h + 1) * HD)
        res = lax.dot_general(q_ref[:, cut], k_ref[:, cut], NT, preferred_element_type=F32) * SCALE
        res = res.astype(BF16)
        for b in range(blocks):
            q_s[b, h * BLOCK_LEN : (h + 1) * BLOCK_LEN, :] = res[b * BLOCK_LEN : (b + 1) * BLOCK_LEN]
    for b in range(blocks):
        at = slice(b * BLOCK_LEN, (b + 1) * BLOCK_LEN)
        rows = jnp.concatenate([own_ref[at, :], left_ref[at, :], right_ref[at, :], far_ref[at, :]], axis=0)
        s = lax.dot_general(q_s[b], rows, NT, preferred_element_type=F32)
        p = jnp.exp2(s - jnp.max(s, axis=1, keepdims=True))
        p = p * (1.0 / jnp.sum(p, axis=1, keepdims=True))
        mixed = jnp.dot(p.astype(BF16), rows, preferred_element_type=F32).astype(BF16)
        for h in range(heads):
            m_s[h, at, :] = mixed[h * BLOCK_LEN : (h + 1) * BLOCK_LEN]
    for h in range(heads):
        at = slice(h * HD, (h + 1) * HD)
        out_ref[:, at] = jnp.dot(m_s[h], v_ref[:, at], preferred_element_type=F32).astype(BF16)


def decode(chunk, queries, pieces, key_weight, value_weight):
    tokens, depth = pieces[0].shape
    width = queries.shape[1]
    heads = width // HD
    blocks = tokens // BLOCK_LEN
    rows = heads * BLOCK_LEN

    def whole(shape):
        return pl.BlockSpec(shape, lambda n: (0, 0))

    return pl.pallas_call(
        decode_kernel,
        grid=(1,),
        out_shape=jax.ShapeDtypeStruct((tokens, width), BF16),
        in_specs=[pl.BlockSpec((tokens, width), lambda n: (chunk, 0))]
        + [whole(pieces[0].shape)] * 4
        + [whole(key_weight.shape)] * 2,
        out_specs=whole((tokens, width)),
        scratch_shapes=[pltpu.VMEM((blocks, rows, depth), BF16), pltpu.VMEM((heads, tokens, depth), BF16)],
        compiler_params=pltpu.CompilerParams(vmem_limit_bytes=VMEM_LIMIT),
        cost_estimate=pl.CostEstimate(
            flops=4 * tokens * depth * (heads * 256 + width), bytes_accessed=7 << 20, transcendentals=blocks * rows * 256
        ),
        name="decode",
    )(queries, *pieces, key_weight, value_weight)


def per_device(
    hidden,
    neighbours,
    block_map,
    enc_key_weight,
    enc_value_weight,
    enc_query_weight,
    enc_out_weight,
    query_weight,
    key_weight,
    value_weight,
    out_weight,
    cotangent,
):
    me = lax.axis_index("tp")
    me_vec = me.reshape(1).astype(jnp.int32)
    core = lax.axis_index("core")
    yg = lax.axis_index("grp") * 2 + lax.axis_index("yhi")
    spot = jnp.stack([lax.axis_index("z"), yg, core, 1 - core]).astype(jnp.int32)
    self_index = lax.axis_index(YZC)
    devices = 32
    local_count, positions, depth = neighbours.shape
    tok_rows, feat = hidden.shape
    chunks = 2
    chunk = tok_rows // chunks

    flat_map = block_map.reshape(devices, local_count)
    owners = flat_map // local_count
    places = flat_map % local_count
    order = jnp.arange(local_count, dtype=jnp.int32)
    send_place = jnp.sum(jnp.where(owners == self_index, places, 0), axis=1)
    my_owners = lax.dynamic_index_in_dim(owners, self_index, 0, keepdims=False)
    everyone = jnp.arange(devices, dtype=jnp.int32)
    back_slot = jnp.sum(jnp.where(my_owners[None, :] == everyone[:, None], order[None, :], 0), axis=1)
    wanted = self_index * local_count + order
    asker = jnp.sum(
        jnp.where(
            flat_map.reshape(1, -1) == wanted[:, None],
            (jnp.arange(devices * local_count, dtype=jnp.int32) // local_count)[None, :],
            0,
        ),
        axis=1,
    )

    ways = (1, -1)
    sent = pick([neighbours], send_place)
    left = lax.ppermute(hidden, "tp", ring(1))
    right = lax.ppermute(hidden, "tp", ring(-1))
    fars = [lax.ppermute(rows_of(left, 0, sent), "tp", ring(1)), lax.ppermute(rows_of(right, 1), "tp", ring(-1))]

    came = lax.all_to_all(sent, YZC, split_axis=0, concat_axis=0, tiled=True)
    mine, enc_queries = take_queries(came, my_owners, enc_query_weight)

    kv_pieces = [
        gather_direct(key_value(i, me_vec, (hidden, left, right), fars[i], enc_key_weight.T, enc_value_weight.T))
        for i in range(chunks)
    ]
    queries = query(me_vec, (hidden, left, right, *fars), query_weight)

    out_all = lax.all_gather(out_weight, YZC, axis=0)

    encoded_parts = []
    encoded_pieces = []
    for i in range(chunks):
        part = encode(i, me_vec, enc_queries, mine, kv_pieces[i], enc_out_weight)
        encoded_parts.append(part.reshape(local_count // chunks, positions, depth))
        encoded_pieces.append(gather_ring(part, ways[i]))

    back = lax.all_to_all(pick(encoded_parts, back_slot), YZC, split_axis=0, concat_axis=0, tiled=True)
    encoded = pick([back], asker)

    own = [decode(i, queries, encoded_pieces[i], key_weight, value_weight) for i in range(chunks)]
    attended = gather_ring(own[0], ways[0]) + gather_ring(own[1], ways[1])
    term = project(*own, out_all)

    others = []
    for half in range(2):
        sums = product_send(half, spot, attended, cotangent, *(() if half else (encoded, term)))
        others.append(lax.ppermute(sums, "core", [(0, 1), (1, 0)]))
    by_z = product_keep(True, 0, spot, attended, cotangent, others[0])
    by_z = [by_z[0]] + [lax.ppermute(by_z[d], "z", ring(d)) for d in (1, 3, 2)]
    by_y = product_keep(False, 1, spot, attended, cotangent, others[1])
    by_y = [by_y[0]] + [lax.ppermute(by_y[d], ("grp", "yhi"), y_pairs(d // 2, d % 2)) for d in (1, 2, 3)]
    projected = lax.psum_scatter(held(term, others[0]), "tp", scatter_dimension=1, tiled=True)
    to_y = stage_sum(True, spot, by_z)
    to_y = [to_y[0]] + [lax.ppermute(to_y[d], ("grp", "yhi"), y_pairs(d // 2, d % 2)) for d in (1, 2, 3)]
    to_z = stage_sum(False, spot, by_y)
    to_z = [to_z[0]] + [lax.ppermute(to_z[d], "z", ring(d)) for d in (1, 3, 2)]
    grad = last_turn(lax.ppermute(middle_sum(to_y + to_z), AXES, owner_pairs()))
    layer_output = (hidden.astype(F32) + projected.astype(F32)).astype(BF16)
    return (layer_output, encoded, grad)


def solution(mesh):
    fine = Mesh(mesh.devices.reshape(2, 4, 2, 2, 4), AXES)
    placed = (
        P(YZC, "tp"),
        P(YZC, "tp", None),
        P(),
        P(None, "tp"),
        P(None, "tp"),
        P(),
        P(),
        P(None, "tp"),
        P(None, "tp"),
        P(None, "tp"),
        P("tp", YZC),
        P(YZC, "tp"),
    )
    return jax.shard_map(
        per_device,
        mesh=fine,
        in_specs=placed,
        out_specs=(P(YZC, "tp"), P(YZC, "tp", None), P("tp", YZC)),
        check_vma=False,
    )
```

```python
import math

import jax
import jax.numpy as jnp
from jax import lax
from jax.experimental import pallas as pl
from jax.experimental.pallas import tpu as pltpu
from jax.sharding import Mesh, PartitionSpec as P

HD = 128
HE = 7
BLOCK_LEN = 64
PICKS = 2
AXES = ("grp", "z", "yhi", "core", "tp")
YZC = ("grp", "z", "yhi", "core")
YZ = ("grp", "z", "yhi")
VMEM_LIMIT = 60 << 20
TAIL_LIMIT = 60 << 20
NEG = -1e30
NT = (((1,), (1,)), ((), ()))
F32 = jnp.float32
SCALE = math.log2(math.e) / math.sqrt(HD)
BF16 = jnp.bfloat16


def ring(step):
    return [(i, (i + step) % 4) for i in range(4)]


def gather_ring(x, way):
    left = lax.ppermute(x, "tp", ring(1))
    right = lax.ppermute(x, "tp", ring(-1))
    far = lax.ppermute(left if way > 0 else right, "tp", ring(way))
    return (x, left, right, far)


def gather_direct(x):
    return (x,) + tuple(lax.ppermute(x, "tp", ring(step)) for step in (1, -1, 2))


STEPS = (0, 3, 1, 2)


def index_of(g, z, y, c, t):
    return (((g * 4 + z) * 2 + y) * 2 + c) * 4 + t


def places():
    return [
        (g, z, y, c, t) for g in range(2) for z in range(4) for y in range(2) for c in range(2) for t in range(4)
    ]


def owner(g, z, y, c, t):
    return index_of(t // 2, 2 * (t % 2) + z % 2, y, c, (t + 2 * g + z // 2) % 4)


def owner_pairs(dg=0, dz=0, dy=0):
    return [(index_of(g, z, y, c, t), owner(g ^ dg, (z + dz) % 4, y ^ dy, c, t)) for g, z, y, c, t in places()]


def y_pairs(dg, dy):
    return [(g * 2 + y, (g ^ dg) * 2 + (y ^ dy)) for g in range(2) for y in range(2)]


def whole_vmem():
    return pl.BlockSpec(memory_space=pltpu.VMEM)


def scalars():
    return pl.BlockSpec(memory_space=pltpu.SMEM)


def anywhere():
    return pl.BlockSpec(memory_space=pl.ANY)


def pick_kernel(tables, index_ref, *refs):
    table_refs, out_ref = refs[:tables], refs[-1]
    size = table_refs[0].shape[0]
    for i in range(out_ref.shape[0]):
        at = index_ref[i]
        if tables == 1:
            out_ref[i] = table_refs[0][at]
        else:
            low = table_refs[0][jnp.minimum(at, size - 1)]
            high = table_refs[1][jnp.maximum(at - size, 0)]
            out_ref[i] = jnp.where(at < size, low, high)


def pick(tables, index, *after):
    shape = index.shape[:1] + tables[0].shape[1:]
    return pl.pallas_call(
        lambda *refs: pick_kernel(len(tables), *refs),
        out_shape=jax.ShapeDtypeStruct(shape, BF16),
        in_specs=[scalars()] + [whole_vmem()] * len(tables) + [anywhere()] * len(after),
        out_specs=whole_vmem(),
        compiler_params=pltpu.CompilerParams(vmem_limit_bytes=VMEM_LIMIT),
        cost_estimate=pl.CostEstimate(flops=0, bytes_accessed=4 * math.prod(shape), transcendentals=0),
        name="pick",
    )(index, *tables, *after)


def take_kernel(index_ref, table_ref, w_ref, out_ref, query_ref):
    size = table_ref.shape[1]
    for i in range(index_ref.shape[0]):
        out_ref[i * size : (i + 1) * size, :] = table_ref[index_ref[i]]
    query_ref[...] = jnp.dot(out_ref[...], w_ref[...], preferred_element_type=F32).astype(BF16)


def take_queries(table, index, weight):
    size, width = table.shape[1:]
    rows = index.shape[0] * size
    return pl.pallas_call(
        take_kernel,
        out_shape=[jax.ShapeDtypeStruct((rows, width), BF16)] * 2,
        in_specs=[scalars()] + [whole_vmem()] * 2,
        out_specs=[whole_vmem()] * 2,
        compiler_params=pltpu.CompilerParams(vmem_limit_bytes=VMEM_LIMIT),
        cost_estimate=pl.CostEstimate(flops=2 * rows * width * width, bytes_accessed=6 << 20, transcendentals=0),
        name="take_queries",
    )(index, table, weight)


def nothing(*refs):
    pass


def held(x, *after):
    return pl.pallas_call(
        nothing,
        out_shape=jax.ShapeDtypeStruct(x.shape, x.dtype),
        in_specs=[anywhere()] * (1 + len(after)),
        out_specs=anywhere(),
        input_output_aliases={0: 0},
        name="held",
    )(x, *after)


def rows_kernel(x_ref, *refs):
    refs[-1][...] = x_ref[...]


def rows_of(x, part, *after):
    rows, width = x.shape[0] // 2, x.shape[1]
    return pl.pallas_call(
        rows_kernel,
        grid=(1,),
        out_shape=jax.ShapeDtypeStruct((rows, width), x.dtype),
        in_specs=[pl.BlockSpec((rows, width), lambda n: (part, 0))] + [anywhere()] * len(after),
        out_specs=pl.BlockSpec((rows, width), lambda n: (0, 0)),
        cost_estimate=pl.CostEstimate(flops=0, bytes_accessed=4 * rows * width, transcendentals=0),
        name="rows_of",
    )(x, *after)


def key_value_kernel(me_ref, own_ref, left_ref, right_ref, far_ref, k_ref, v_ref, out_ref):
    me = me_ref[0]
    width = own_ref.shape[1]
    part = k_ref.shape[0]
    for n, w_ref in enumerate((k_ref, v_ref)):
        total = None
        for step, ref in zip(STEPS, (own_ref, left_ref, right_ref, far_ref)):
            at = pl.ds(pl.multiple_of((me + step) % 4 * width, 128), width)
            term = lax.dot_general(w_ref[:, at], ref[...], NT, preferred_element_type=F32)
            total = term if total is None else total + term
        out_ref[n * part : (n + 1) * part, :] = total.astype(BF16)


def key_value(chunk, me, pieces, far, key_weight, value_weight):
    rows, width = far.shape
    part = key_weight.shape[0]

    def whole(shape):
        return pl.BlockSpec(shape, lambda n: (0, 0))

    return pl.pallas_call(
        key_value_kernel,
        grid=(1,),
        out_shape=jax.ShapeDtypeStruct((2 * part, rows), BF16),
        in_specs=[scalars()]
        + [pl.BlockSpec((rows, width), lambda n: (chunk, 0))] * 3
        + [whole(far.shape), whole(key_weight.shape), whole(key_weight.shape)],
        out_specs=whole((2 * part, rows)),
        compiler_params=pltpu.CompilerParams(vmem_limit_bytes=VMEM_LIMIT),
        cost_estimate=pl.CostEstimate(flops=4 * rows * 4096 * part, bytes_accessed=6 << 20, transcendentals=0),
        name="key_value",
    )(me, *pieces, far, key_weight, value_weight)


def query_kernel(me_ref, own_ref, left_ref, right_ref, far_top_ref, far_bottom_ref, w_ref, out_ref, sum_s):
    step = pl.program_id(0)
    half = far_top_ref.shape[0]

    def term(ref):
        return jnp.dot(ref[...], w_ref[...], preferred_element_type=F32)

    @pl.when(step == 0)
    def _():
        sum_s[...] = term(own_ref)

    @pl.when(step == 1)
    def _():
        sum_s[...] += term(left_ref)

    @pl.when(step == 2)
    def _():
        sum_s[...] += term(right_ref)

    @pl.when(step == 3)
    def _():
        out_ref[:half] = (sum_s[:half] + term(far_top_ref)).astype(BF16)
        out_ref[half:] = (sum_s[half:] + term(far_bottom_ref)).astype(BF16)


def step_of(n):
    return (n == 1) * 3 + (n == 2) * 1 + (n == 3) * 2


def query(me, pieces, weight):
    rows, part = pieces[0].shape
    width = weight.shape[1]
    return pl.pallas_call(
        query_kernel,
        grid_spec=pltpu.PrefetchScalarGridSpec(
            num_scalar_prefetch=1,
            grid=(4,),
            in_specs=[pl.BlockSpec(piece.shape, lambda n, me: (0, 0)) for piece in pieces]
            + [pl.BlockSpec((part, width), lambda n, me: ((me[0] + step_of(n)) % 4, 0))],
            out_specs=pl.BlockSpec((rows, width), lambda n, me: (0, 0)),
            scratch_shapes=[pltpu.VMEM((rows, width), F32)],
        ),
        out_shape=jax.ShapeDtypeStruct((rows, width), BF16),
        compiler_params=pltpu.CompilerParams(vmem_limit_bytes=VMEM_LIMIT),
        cost_estimate=pl.CostEstimate(flops=8 * rows * width * part, bytes_accessed=13 << 20, transcendentals=0),
        name="query",
    )(me, *pieces, weight)


def project_kernel(top_ref, bottom_ref, w_ref, out_ref):
    attended = jnp.concatenate([top_ref[...], bottom_ref[...]], axis=0)
    for k in range(0, w_ref.shape[0], 2):
        weight = jnp.concatenate([w_ref[k], w_ref[k + 1]], axis=1)
        out_ref[:, k * HD : (k + 2) * HD] = jnp.dot(attended, weight, preferred_element_type=F32).astype(BF16)


def project(top, bottom, out_all, *after):
    rows, feat = top.shape
    count = out_all.shape[0]
    step = 4
    return pl.pallas_call(
        lambda *refs: project_kernel(*refs[:3], refs[-1]),
        grid=(count // step,),
        out_shape=jax.ShapeDtypeStruct((2 * rows, count * HD), BF16),
        in_specs=[pl.BlockSpec(top.shape, lambda n: (0, 0))] * 2
        + [pl.BlockSpec((step, feat, HD), lambda n: (n, 0, 0))]
        + [anywhere()] * len(after),
        out_specs=pl.BlockSpec((2 * rows, step * HD), lambda n: (0, n)),
        compiler_params=pltpu.CompilerParams(vmem_limit_bytes=VMEM_LIMIT),
        cost_estimate=pl.CostEstimate(flops=4 * rows * feat * count * HD, bytes_accessed=14 << 20, transcendentals=0),
        name="project",
    )(top, bottom, out_all, *after)


def product_kernel(place, spot_ref, *refs):
    piece_refs, cot_ref, store, cot_s = refs[:8], refs[8], refs[9], refs[-1]
    core = spot_ref[place]
    for p in range(4):
        at = pl.ds(pl.multiple_of((2 * p + core) * HD, HD), HD)
        cot_s[p * HD : (p + 1) * HD, :] = cot_ref[:, at].T
    for r, step in enumerate(STEPS):
        both = jnp.concatenate([piece_refs[r][...], piece_refs[4 + r][...]], axis=0)
        res = jnp.dot(cot_s[...], both, preferred_element_type=F32)
        for p in range(4):
            store[step // 2 * 8 + step % 2 * 4 + p] = res[p * HD : (p + 1) * HD].astype(store.dtype)


def keep_kernel(by_z, spot_ref, *refs):
    came_ref, outs, (sums, cot_s) = refs[9], refs[-6:-2], refs[-2:]
    product_kernel(2, spot_ref, *refs[:9], sums, cot_s)
    z, yg = spot_ref[0], spot_ref[1]
    for d in range(4):
        for k in range(4):
            if by_z:
                at = (k // 2 * 4 + (z + d) % 4) * 2 + k % 2
            else:
                at = ((yg ^ d) // 2 * 4 + k) * 2 + (yg ^ d) % 2
            outs[d][k] = (sums[at] + came_ref[at].astype(F32)).astype(BF16)


def product_call(kernel, name, half, spot, pieces, cot, extra, extra_specs, out_shape, out_specs, scratch):
    feat = pieces[0].shape[1] // 2
    tokens = cot.shape[0]
    cut = pl.BlockSpec((pieces[0].shape[0], feat), lambda n: (0, half))
    return pl.pallas_call(
        kernel,
        grid=(1,),
        out_shape=out_shape,
        in_specs=[scalars()] + [cut] * 8 + [pl.BlockSpec(cot.shape, lambda n: (0, 0))] + extra_specs,
        out_specs=out_specs,
        scratch_shapes=scratch + [pltpu.VMEM((cot.shape[1] // 2, tokens), BF16)],
        compiler_params=pltpu.CompilerParams(vmem_limit_bytes=TAIL_LIMIT),
        cost_estimate=pl.CostEstimate(
            flops=cot.shape[1] * tokens * 4 * feat, bytes_accessed=7 << 20, transcendentals=0
        ),
        name=name,
    )(spot, *pieces, cot, *extra)


def product_send(half, spot, pieces, cot, *after):
    shape = (16, HD, pieces[0].shape[1] // 2)

    def kernel(*refs):
        product_kernel(3, *refs[:10], *refs[10 + len(after) :])

    return product_call(
        kernel,
        "product_send",
        half,
        spot,
        pieces,
        cot,
        after,
        [anywhere()] * len(after),
        jax.ShapeDtypeStruct(shape, BF16),
        pl.BlockSpec(shape, lambda n: (0, 0, 0)),
        [],
    )


def product_keep(by_z, half, spot, pieces, cot, came, *after):
    _, rows, feat = came.shape
    return product_call(
        lambda *refs: keep_kernel(by_z, *refs),
        "product_keep",
        half,
        spot,
        pieces,
        cot,
        (came, *after),
        [pl.BlockSpec(came.shape, lambda n: (0, 0, 0))] + [anywhere()] * len(after),
        [jax.ShapeDtypeStruct((4, rows, feat), BF16)] * 4,
        [pl.BlockSpec((4, rows, feat), lambda n: (0, 0, 0))] * 4,
        [pltpu.VMEM(came.shape, F32)],
    )


def stage_kernel(by_z, at_ref, a_ref, b_ref, c_ref, d_ref, *outs):
    z, yg = at_ref[0], at_ref[1]
    for d in range(4):
        k = yg ^ d if by_z else (z + d) % 4
        total = a_ref[k].astype(F32) + b_ref[k].astype(F32) + c_ref[k].astype(F32) + d_ref[k].astype(F32)
        outs[d][...] = total.astype(BF16)


def stage_sum(by_z, at, parts, *after):
    _, rows, half = parts[0].shape
    step = rows // 2
    return pl.pallas_call(
        lambda *refs: stage_kernel(by_z, *refs[:5], *refs[5 + len(after) :]),
        grid=(2,),
        out_shape=[jax.ShapeDtypeStruct((rows, half), BF16)] * 4,
        in_specs=[scalars()]
        + [pl.BlockSpec((4, step, half), lambda n: (0, n, 0))] * 4
        + [anywhere()] * len(after),
        out_specs=[pl.BlockSpec((step, half), lambda n: (n, 0))] * 4,
        compiler_params=pltpu.CompilerParams(vmem_limit_bytes=TAIL_LIMIT),
        cost_estimate=pl.CostEstimate(flops=16 * rows * half, bytes_accessed=3 << 20, transcendentals=0),
        name="stage_sum",
    )(at, *parts, *after)


def middle_kernel(*refs):
    out_ref = refs[-1]
    rows = refs[0].shape[0]
    for i in range(2):
        total = refs[4 * i][...].astype(F32)
        for ref in refs[4 * i + 1 : 4 * i + 4]:
            total = total + ref[...].astype(F32)
        out_ref[i * rows : (i + 1) * rows, :] = total.astype(BF16)


def middle_sum(parts, *after):
    rows, half = parts[0].shape
    return pl.pallas_call(
        middle_kernel,
        out_shape=jax.ShapeDtypeStruct((2 * rows, half), BF16),
        in_specs=[whole_vmem()] * 8 + [anywhere()] * len(after),
        out_specs=whole_vmem(),
        cost_estimate=pl.CostEstimate(flops=8 * rows * half, bytes_accessed=2 << 20, transcendentals=0),
        name="middle_sum",
    )(*parts, *after)


def last_kernel(x_ref, out_ref):
    rows, half = x_ref.shape
    for i in range(2):
        cut = slice(i * (rows // 2), (i + 1) * (rows // 2))
        out_ref[i * half : (i + 1) * half, :] = x_ref[cut, :].astype(F32).T


def last_turn(x):
    rows, half = x.shape
    return pl.pallas_call(
        last_kernel,
        out_shape=jax.ShapeDtypeStruct((2 * half, rows // 2), F32),
        in_specs=[whole_vmem()],
        out_specs=whole_vmem(),
        cost_estimate=pl.CostEstimate(flops=rows * half, bytes_accessed=1 << 20, transcendentals=0),
        name="last_turn",
    )(x)


def encode_kernel(me_ref, q_ref, nb_ref, own_ref, left_ref, right_ref, far_ref, w_ref, out_ref, k_s, v_s, m_s):
    part = own_ref.shape[0] // 2
    me = me_ref[0]
    for step, ref in zip(STEPS, (own_ref, left_ref, right_ref, far_ref)):
        at = pl.ds(pl.multiple_of((me + step) % 4 * part, 32), part)
        k_s[at, :] = ref[:part, :]
        v_s[at, :] = ref[part:, :]
    rows, cols = q_ref.shape[0], k_s.shape[1]
    same = (
        lax.broadcasted_iota(jnp.int32, (rows, cols), 0) // BLOCK_LEN
        == lax.broadcasted_iota(jnp.int32, (rows, cols), 1) // BLOCK_LEN
    )
    for h in range(HE):
        at = slice(h * HD, (h + 1) * HD)
        s = jnp.dot(q_ref[:, at], k_s[at, :], preferred_element_type=F32) * SCALE
        s = jnp.where(same, s, NEG)
        p = jnp.exp2(s - jnp.max(s, axis=1, keepdims=True))
        p = p * (1.0 / jnp.sum(p, axis=1, keepdims=True))
        m_s[:, at] = lax.dot_general(p.astype(BF16), v_s[at, :], NT, preferred_element_type=F32).astype(BF16)
    out_ref[...] = (
        nb_ref[...].astype(F32) + jnp.dot(m_s[...], w_ref[...], preferred_element_type=F32)
    ).astype(BF16)


def encode(chunk, me, queries, neighbours, pieces, weight):
    width = neighbours.shape[1]
    rows = neighbours.shape[0] // 2
    tokens = pieces[0].shape[1]

    def whole(shape):
        return pl.BlockSpec(shape, lambda n: (0, 0))

    part = pl.BlockSpec((rows, width), lambda n: (chunk, 0))
    return pl.pallas_call(
        encode_kernel,
        grid=(1,),
        out_shape=jax.ShapeDtypeStruct((rows, width), BF16),
        in_specs=[scalars(), part, part] + [whole(pieces[0].shape)] * 4 + [whole(weight.shape)],
        out_specs=whole((rows, width)),
        scratch_shapes=[
            pltpu.VMEM((width, tokens), BF16),
            pltpu.VMEM((width, tokens), BF16),
            pltpu.VMEM((rows, width), BF16),
        ],
        compiler_params=pltpu.CompilerParams(vmem_limit_bytes=VMEM_LIMIT),
        cost_estimate=pl.CostEstimate(
            flops=2 * rows * width * (width + 2 * tokens), bytes_accessed=4 << 20, transcendentals=HE * rows * tokens
        ),
        name="encode",
    )(me, queries, neighbours, *pieces, weight)


def decode_kernel(q_ref, own_ref, left_ref, right_ref, far_ref, k_ref, v_ref, out_ref, q_s, m_s):
    heads, tokens, _ = m_s.shape
    blocks = tokens // BLOCK_LEN
    for h in range(heads):
        cut = slice(h * HD, (h + 1) * HD)
        res = lax.dot_general(q_ref[:, cut], k_ref[:, cut], NT, preferred_element_type=F32) * SCALE
        res = res.astype(BF16)
        for b in range(blocks):
            q_s[b, h * BLOCK_LEN : (h + 1) * BLOCK_LEN, :] = res[b * BLOCK_LEN : (b + 1) * BLOCK_LEN]
    for b in range(blocks):
        at = slice(b * BLOCK_LEN, (b + 1) * BLOCK_LEN)
        rows = jnp.concatenate([own_ref[at, :], left_ref[at, :], right_ref[at, :], far_ref[at, :]], axis=0)
        s = lax.dot_general(q_s[b], rows, NT, preferred_element_type=F32)
        p = jnp.exp2(s - jnp.max(s, axis=1, keepdims=True))
        p = p * (1.0 / jnp.sum(p, axis=1, keepdims=True))
        mixed = jnp.dot(p.astype(BF16), rows, preferred_element_type=F32).astype(BF16)
        for h in range(heads):
            m_s[h, at, :] = mixed[h * BLOCK_LEN : (h + 1) * BLOCK_LEN]
    for h in range(heads):
        at = slice(h * HD, (h + 1) * HD)
        out_ref[:, at] = jnp.dot(m_s[h], v_ref[:, at], preferred_element_type=F32).astype(BF16)


def decode(chunk, queries, pieces, key_weight, value_weight):
    tokens, depth = pieces[0].shape
    width = queries.shape[1]
    heads = width // HD
    blocks = tokens // BLOCK_LEN
    rows = heads * BLOCK_LEN

    def whole(shape):
        return pl.BlockSpec(shape, lambda n: (0, 0))

    return pl.pallas_call(
        decode_kernel,
        grid=(1,),
        out_shape=jax.ShapeDtypeStruct((tokens, width), BF16),
        in_specs=[pl.BlockSpec((tokens, width), lambda n: (chunk, 0))]
        + [whole(pieces[0].shape)] * 4
        + [whole(key_weight.shape)] * 2,
        out_specs=whole((tokens, width)),
        scratch_shapes=[pltpu.VMEM((blocks, rows, depth), BF16), pltpu.VMEM((heads, tokens, depth), BF16)],
        compiler_params=pltpu.CompilerParams(vmem_limit_bytes=VMEM_LIMIT),
        cost_estimate=pl.CostEstimate(
            flops=4 * tokens * depth * (heads * 256 + width), bytes_accessed=7 << 20, transcendentals=blocks * rows * 256
        ),
        name="decode",
    )(queries, *pieces, key_weight, value_weight)


def per_device(
    hidden,
    neighbours,
    block_map,
    enc_key_weight,
    enc_value_weight,
    enc_query_weight,
    enc_out_weight,
    query_weight,
    key_weight,
    value_weight,
    out_weight,
    cotangent,
):
    me = lax.axis_index("tp")
    me_vec = me.reshape(1).astype(jnp.int32)
    core = lax.axis_index("core")
    yg = lax.axis_index("grp") * 2 + lax.axis_index("yhi")
    spot = jnp.stack([lax.axis_index("z"), yg, core, 1 - core]).astype(jnp.int32)
    self_index = lax.axis_index(YZC)
    devices = 32
    local_count, positions, depth = neighbours.shape
    tok_rows, feat = hidden.shape
    chunks = 2
    chunk = tok_rows // chunks

    flat_map = block_map.reshape(devices, local_count)
    owners = flat_map // local_count
    places = flat_map % local_count
    order = jnp.arange(local_count, dtype=jnp.int32)
    send_place = jnp.sum(jnp.where(owners == self_index, places, 0), axis=1)
    my_owners = lax.dynamic_index_in_dim(owners, self_index, 0, keepdims=False)
    everyone = jnp.arange(devices, dtype=jnp.int32)
    back_slot = jnp.sum(jnp.where(my_owners[None, :] == everyone[:, None], order[None, :], 0), axis=1)
    wanted = self_index * local_count + order
    asker = jnp.sum(
        jnp.where(
            flat_map.reshape(1, -1) == wanted[:, None],
            (jnp.arange(devices * local_count, dtype=jnp.int32) // local_count)[None, :],
            0,
        ),
        axis=1,
    )

    ways = (1, -1)
    sent = pick([neighbours], send_place)
    left = lax.ppermute(hidden, "tp", ring(1))
    right = lax.ppermute(hidden, "tp", ring(-1))
    fars = [lax.ppermute(rows_of(left, 0, sent), "tp", ring(1)), lax.ppermute(rows_of(right, 1), "tp", ring(-1))]

    came = lax.all_to_all(sent, YZC, split_axis=0, concat_axis=0, tiled=True)
    mine, enc_queries = take_queries(came, my_owners, enc_query_weight)

    kv_pieces = [
        gather_direct(key_value(i, me_vec, (hidden, left, right), fars[i], enc_key_weight.T, enc_value_weight.T))
        for i in range(chunks)
    ]
    queries = query(me_vec, (hidden, left, right, *fars), query_weight)

    out_all = lax.all_gather(out_weight, YZC, axis=0)

    encoded_parts = []
    encoded_pieces = []
    for i in range(chunks):
        part = encode(i, me_vec, enc_queries, mine, kv_pieces[i], enc_out_weight)
        encoded_parts.append(part.reshape(local_count // chunks, positions, depth))
        encoded_pieces.append(gather_ring(part, ways[i]))

    back = lax.all_to_all(pick(encoded_parts, back_slot), YZC, split_axis=0, concat_axis=0, tiled=True)
    encoded = pick([back], asker)

    own = [decode(i, queries, encoded_pieces[i], key_weight, value_weight) for i in range(chunks)]
    attended = gather_ring(own[0], ways[0]) + gather_ring(own[1], ways[1])
    term = project(*own, out_all)

    others, sent_sums = [], []
    for half in range(2):
        sums = product_send(half, spot, attended, cotangent, *(() if half else (encoded, term)))
        sent_sums.append(sums)
        others.append(lax.ppermute(sums, "core", [(0, 1), (1, 0)]))
    by_z = product_keep(True, 0, spot, attended, cotangent, others[0])
    by_z = [by_z[0]] + [lax.ppermute(by_z[d], "z", ring(d)) for d in (1, 3, 2)]
    by_y = product_keep(False, 1, spot, attended, cotangent, others[1])
    by_y = [by_y[0]] + [lax.ppermute(by_y[d], ("grp", "yhi"), y_pairs(d // 2, d % 2)) for d in (1, 2, 3)]
    projected = lax.psum_scatter(held(term, sent_sums[0]), "tp", scatter_dimension=1, tiled=True)
    to_y = stage_sum(True, spot, by_z)
    to_y = [to_y[0]] + [lax.ppermute(to_y[d], ("grp", "yhi"), y_pairs(d // 2, d % 2)) for d in (1, 2, 3)]
    to_z = stage_sum(False, spot, by_y)
    to_z = [to_z[0]] + [lax.ppermute(to_z[d], "z", ring(d)) for d in (1, 3, 2)]
    layer_output = (hidden.astype(F32) + projected.astype(F32)).astype(BF16)
    grad = last_turn(lax.ppermute(middle_sum(to_y + to_z, layer_output), AXES, owner_pairs()))
    return (layer_output, encoded, grad)


def solution(mesh):
    fine = Mesh(mesh.devices.reshape(2, 4, 2, 2, 4), AXES)
    placed = (
        P(YZC, "tp"),
        P(YZC, "tp", None),
        P(),
        P(None, "tp"),
        P(None, "tp"),
        P(),
        P(),
        P(None, "tp"),
        P(None, "tp"),
        P(None, "tp"),
        P("tp", YZC),
        P(YZC, "tp"),
    )
    return jax.shard_map(
        per_device,
        mesh=fine,
        in_specs=placed,
        out_specs=(P(YZC, "tp"), P(YZC, "tp", None), P("tp", YZC)),
        check_vma=False,
    )
```

```python
import math

import jax
import jax.numpy as jnp
from jax import lax
from jax.experimental import pallas as pl
from jax.experimental.pallas import tpu as pltpu
from jax.sharding import Mesh, PartitionSpec as P

HD = 128
HE = 7
BLOCK_LEN = 64
PICKS = 2
AXES = ("grp", "z", "yhi", "core", "tp")
YZC = ("grp", "z", "yhi", "core")
YZ = ("grp", "z", "yhi")
VMEM_LIMIT = 60 << 20
TAIL_LIMIT = 60 << 20
NEG = -1e30
NT = (((1,), (1,)), ((), ()))
F32 = jnp.float32
SCALE = math.log2(math.e) / math.sqrt(HD)
BF16 = jnp.bfloat16


def ring(step):
    return [(i, (i + step) % 4) for i in range(4)]


def gather_ring(x, way):
    left = lax.ppermute(x, "tp", ring(1))
    right = lax.ppermute(x, "tp", ring(-1))
    far = lax.ppermute(left if way > 0 else right, "tp", ring(way))
    return (x, left, right, far)


def gather_direct(x):
    return (x,) + tuple(lax.ppermute(x, "tp", ring(step)) for step in (1, -1, 2))


STEPS = (0, 3, 1, 2)


def index_of(g, z, y, c, t):
    return (((g * 4 + z) * 2 + y) * 2 + c) * 4 + t


def places():
    return [
        (g, z, y, c, t) for g in range(2) for z in range(4) for y in range(2) for c in range(2) for t in range(4)
    ]


def owner(g, z, y, c, t):
    return index_of(t // 2, 2 * (t % 2) + z % 2, y, c, (t + 2 * g + z // 2) % 4)


def owner_pairs(dg=0, dz=0, dy=0):
    return [(index_of(g, z, y, c, t), owner(g ^ dg, (z + dz) % 4, y ^ dy, c, t)) for g, z, y, c, t in places()]


def y_pairs(dg, dy):
    return [(g * 2 + y, (g ^ dg) * 2 + (y ^ dy)) for g in range(2) for y in range(2)]


def whole_vmem():
    return pl.BlockSpec(memory_space=pltpu.VMEM)


def scalars():
    return pl.BlockSpec(memory_space=pltpu.SMEM)


def anywhere():
    return pl.BlockSpec(memory_space=pl.ANY)


def pick_kernel(tables, index_ref, *refs):
    table_refs, out_ref = refs[:tables], refs[-1]
    size = table_refs[0].shape[0]
    for i in range(out_ref.shape[0]):
        at = index_ref[i]
        if tables == 1:
            out_ref[i] = table_refs[0][at]
        else:
            low = table_refs[0][jnp.minimum(at, size - 1)]
            high = table_refs[1][jnp.maximum(at - size, 0)]
            out_ref[i] = jnp.where(at < size, low, high)


def pick(tables, index, *after):
    shape = index.shape[:1] + tables[0].shape[1:]
    return pl.pallas_call(
        lambda *refs: pick_kernel(len(tables), *refs),
        out_shape=jax.ShapeDtypeStruct(shape, BF16),
        in_specs=[scalars()] + [whole_vmem()] * len(tables) + [anywhere()] * len(after),
        out_specs=whole_vmem(),
        compiler_params=pltpu.CompilerParams(vmem_limit_bytes=VMEM_LIMIT),
        cost_estimate=pl.CostEstimate(flops=0, bytes_accessed=4 * math.prod(shape), transcendentals=0),
        name="pick",
    )(index, *tables, *after)


def take_kernel(index_ref, table_ref, w_ref, out_ref, query_ref):
    size = table_ref.shape[1]
    for i in range(index_ref.shape[0]):
        out_ref[i * size : (i + 1) * size, :] = table_ref[index_ref[i]]
    query_ref[...] = jnp.dot(out_ref[...], w_ref[...], preferred_element_type=F32).astype(BF16)


def take_queries(table, index, weight):
    size, width = table.shape[1:]
    rows = index.shape[0] * size
    return pl.pallas_call(
        take_kernel,
        out_shape=[jax.ShapeDtypeStruct((rows, width), BF16)] * 2,
        in_specs=[scalars()] + [whole_vmem()] * 2,
        out_specs=[whole_vmem()] * 2,
        compiler_params=pltpu.CompilerParams(vmem_limit_bytes=VMEM_LIMIT),
        cost_estimate=pl.CostEstimate(flops=2 * rows * width * width, bytes_accessed=6 << 20, transcendentals=0),
        name="take_queries",
    )(index, table, weight)


def nothing(*refs):
    pass


def held(x, *after):
    return pl.pallas_call(
        nothing,
        out_shape=jax.ShapeDtypeStruct(x.shape, x.dtype),
        in_specs=[anywhere()] * (1 + len(after)),
        out_specs=anywhere(),
        input_output_aliases={0: 0},
        name="held",
    )(x, *after)


def rows_kernel(x_ref, *refs):
    refs[-1][...] = x_ref[...]


def rows_of(x, part, *after):
    rows, width = x.shape[0] // 2, x.shape[1]
    return pl.pallas_call(
        rows_kernel,
        grid=(1,),
        out_shape=jax.ShapeDtypeStruct((rows, width), x.dtype),
        in_specs=[pl.BlockSpec((rows, width), lambda n: (part, 0))] + [anywhere()] * len(after),
        out_specs=pl.BlockSpec((rows, width), lambda n: (0, 0)),
        cost_estimate=pl.CostEstimate(flops=0, bytes_accessed=4 * rows * width, transcendentals=0),
        name="rows_of",
    )(x, *after)


def key_value_kernel(me_ref, own_ref, left_ref, right_ref, far_ref, k_ref, v_ref, out_ref):
    me = me_ref[0]
    width = own_ref.shape[1]
    part = k_ref.shape[0]
    for n, w_ref in enumerate((k_ref, v_ref)):
        total = None
        for step, ref in zip(STEPS, (own_ref, left_ref, right_ref, far_ref)):
            at = pl.ds(pl.multiple_of((me + step) % 4 * width, 128), width)
            term = lax.dot_general(w_ref[:, at], ref[...], NT, preferred_element_type=F32)
            total = term if total is None else total + term
        out_ref[n * part : (n + 1) * part, :] = total.astype(BF16)


def key_value(chunk, me, pieces, far, key_weight, value_weight, *after):
    rows, width = far.shape
    part = key_weight.shape[0]

    def whole(shape):
        return pl.BlockSpec(shape, lambda n: (0, 0))

    return pl.pallas_call(
        lambda *refs: key_value_kernel(*refs[:7], refs[-1]),
        grid=(1,),
        out_shape=jax.ShapeDtypeStruct((2 * part, rows), BF16),
        in_specs=[scalars()]
        + [pl.BlockSpec((rows, width), lambda n: (chunk, 0))] * 3
        + [whole(far.shape), whole(key_weight.shape), whole(key_weight.shape)]
        + [anywhere()] * len(after),
        out_specs=whole((2 * part, rows)),
        compiler_params=pltpu.CompilerParams(vmem_limit_bytes=VMEM_LIMIT),
        cost_estimate=pl.CostEstimate(flops=4 * rows * 4096 * part, bytes_accessed=6 << 20, transcendentals=0),
        name="key_value",
    )(me, *pieces, far, key_weight, value_weight, *after)


def query_kernel(count, based, me_ref, *refs):
    piece_refs, w_ref, out_ref, sum_s = refs[:count], refs[count], refs[-2], refs[-1]
    step = pl.program_id(0)

    @pl.when(step == 0)
    def _():
        sum_s[...] = refs[count + 1][...] if based else jnp.zeros(sum_s.shape, F32)

    if piece_refs[0].shape[0] == sum_s.shape[0]:
        for k, ref in enumerate(piece_refs):

            @pl.when(step == k)
            def _(ref=ref):
                sum_s[...] += jnp.dot(ref[...], w_ref[...], preferred_element_type=F32)
    else:
        half = piece_refs[0].shape[0]
        for k, ref in enumerate(piece_refs):
            cut = slice(k * half, (k + 1) * half)
            sum_s[cut, :] += jnp.dot(ref[...], w_ref[...], preferred_element_type=F32)

    @pl.when(step == pl.num_programs(0) - 1)
    def _():
        out_ref[...] = sum_s[...].astype(out_ref.dtype)


def query(me, steps, pieces, weight, base, dtype):
    part = pieces[0].shape[1]
    rows = pieces[0].shape[0] * len(pieces) // len(steps)
    width = weight.shape[1]
    first, second = steps[0], steps[-1]
    bases = [] if base is None else [base]

    def row_block(n, me):
        return ((me[0] + first + n * (second - first) + 4) % 4, 0)

    return pl.pallas_call(
        lambda *refs: query_kernel(len(pieces), len(bases), *refs),
        grid_spec=pltpu.PrefetchScalarGridSpec(
            num_scalar_prefetch=1,
            grid=(len(steps),),
            in_specs=[pl.BlockSpec(piece.shape, lambda n, me: (0, 0)) for piece in pieces]
            + [pl.BlockSpec((part, width), row_block)]
            + [pl.BlockSpec((rows, width), lambda n, me: (0, 0)) for _ in bases],
            out_specs=pl.BlockSpec((rows, width), lambda n, me: (0, 0)),
            scratch_shapes=[pltpu.VMEM((rows, width), F32)],
        ),
        out_shape=jax.ShapeDtypeStruct((rows, width), dtype),
        compiler_params=pltpu.CompilerParams(vmem_limit_bytes=VMEM_LIMIT),
        cost_estimate=pl.CostEstimate(
            flops=2 * rows * width * part * len(steps), bytes_accessed=6 << 20, transcendentals=0
        ),
        name="query",
    )(me, *pieces, weight, *bases)


def project_kernel(top_ref, bottom_ref, w_ref, out_ref):
    attended = jnp.concatenate([top_ref[...], bottom_ref[...]], axis=0)
    for k in range(0, w_ref.shape[0], 2):
        weight = jnp.concatenate([w_ref[k], w_ref[k + 1]], axis=1)
        out_ref[:, k * HD : (k + 2) * HD] = jnp.dot(attended, weight, preferred_element_type=F32).astype(BF16)


def project(top, bottom, out_all, *after):
    rows, feat = top.shape
    count = out_all.shape[0]
    step = 4
    return pl.pallas_call(
        lambda *refs: project_kernel(*refs[:3], refs[-1]),
        grid=(count // step,),
        out_shape=jax.ShapeDtypeStruct((2 * rows, count * HD), BF16),
        in_specs=[pl.BlockSpec(top.shape, lambda n: (0, 0))] * 2
        + [pl.BlockSpec((step, feat, HD), lambda n: (n, 0, 0))]
        + [anywhere()] * len(after),
        out_specs=pl.BlockSpec((2 * rows, step * HD), lambda n: (0, n)),
        compiler_params=pltpu.CompilerParams(vmem_limit_bytes=VMEM_LIMIT),
        cost_estimate=pl.CostEstimate(flops=4 * rows * feat * count * HD, bytes_accessed=14 << 20, transcendentals=0),
        name="project",
    )(top, bottom, out_all, *after)


def product_kernel(place, spot_ref, *refs):
    piece_refs, cot_ref, store, cot_s = refs[:8], refs[8], refs[9], refs[-1]
    core = spot_ref[place]
    for p in range(4):
        at = pl.ds(pl.multiple_of((2 * p + core) * HD, HD), HD)
        cot_s[p * HD : (p + 1) * HD, :] = cot_ref[:, at].T
    for r, step in enumerate(STEPS):
        both = jnp.concatenate([piece_refs[r][...], piece_refs[4 + r][...]], axis=0)
        res = jnp.dot(cot_s[...], both, preferred_element_type=F32)
        for p in range(4):
            store[step // 2 * 8 + step % 2 * 4 + p] = res[p * HD : (p + 1) * HD].astype(store.dtype)


def keep_kernel(by_z, spot_ref, *refs):
    came_ref, outs, (sums, cot_s) = refs[9], refs[-6:-2], refs[-2:]
    product_kernel(2, spot_ref, *refs[:9], sums, cot_s)
    z, yg = spot_ref[0], spot_ref[1]
    for d in range(4):
        for k in range(4):
            if by_z:
                at = (k // 2 * 4 + (z + d) % 4) * 2 + k % 2
            else:
                at = ((yg ^ d) // 2 * 4 + k) * 2 + (yg ^ d) % 2
            outs[d][k] = (sums[at] + came_ref[at].astype(F32)).astype(BF16)


def product_call(kernel, name, half, spot, pieces, cot, extra, extra_specs, out_shape, out_specs, scratch):
    feat = pieces[0].shape[1] // 2
    tokens = cot.shape[0]
    cut = pl.BlockSpec((pieces[0].shape[0], feat), lambda n: (0, half))
    return pl.pallas_call(
        kernel,
        grid=(1,),
        out_shape=out_shape,
        in_specs=[scalars()] + [cut] * 8 + [pl.BlockSpec(cot.shape, lambda n: (0, 0))] + extra_specs,
        out_specs=out_specs,
        scratch_shapes=scratch + [pltpu.VMEM((cot.shape[1] // 2, tokens), BF16)],
        compiler_params=pltpu.CompilerParams(vmem_limit_bytes=TAIL_LIMIT),
        cost_estimate=pl.CostEstimate(
            flops=cot.shape[1] * tokens * 4 * feat, bytes_accessed=7 << 20, transcendentals=0
        ),
        name=name,
    )(spot, *pieces, cot, *extra)


def product_send(half, spot, pieces, cot, *after):
    shape = (16, HD, pieces[0].shape[1] // 2)

    def kernel(*refs):
        product_kernel(3, *refs[:10], *refs[10 + len(after) :])

    return product_call(
        kernel,
        "product_send",
        half,
        spot,
        pieces,
        cot,
        after,
        [anywhere()] * len(after),
        jax.ShapeDtypeStruct(shape, BF16),
        pl.BlockSpec(shape, lambda n: (0, 0, 0)),
        [],
    )


def product_keep(by_z, half, spot, pieces, cot, came, *after):
    _, rows, feat = came.shape
    return product_call(
        lambda *refs: keep_kernel(by_z, *refs),
        "product_keep",
        half,
        spot,
        pieces,
        cot,
        (came, *after),
        [pl.BlockSpec(came.shape, lambda n: (0, 0, 0))] + [anywhere()] * len(after),
        [jax.ShapeDtypeStruct((4, rows, feat), BF16)] * 4,
        [pl.BlockSpec((4, rows, feat), lambda n: (0, 0, 0))] * 4,
        [pltpu.VMEM(came.shape, F32)],
    )


def stage_kernel(by_z, at_ref, a_ref, b_ref, c_ref, d_ref, *outs):
    z, yg = at_ref[0], at_ref[1]
    for d in range(4):
        k = yg ^ d if by_z else (z + d) % 4
        total = a_ref[k].astype(F32) + b_ref[k].astype(F32) + c_ref[k].astype(F32) + d_ref[k].astype(F32)
        outs[d][...] = total.astype(BF16)


def stage_sum(by_z, at, parts, *after):
    _, rows, half = parts[0].shape
    step = rows // 2
    return pl.pallas_call(
        lambda *refs: stage_kernel(by_z, *refs[:5], *refs[5 + len(after) :]),
        grid=(2,),
        out_shape=[jax.ShapeDtypeStruct((rows, half), BF16)] * 4,
        in_specs=[scalars()]
        + [pl.BlockSpec((4, step, half), lambda n: (0, n, 0))] * 4
        + [anywhere()] * len(after),
        out_specs=[pl.BlockSpec((step, half), lambda n: (n, 0))] * 4,
        compiler_params=pltpu.CompilerParams(vmem_limit_bytes=TAIL_LIMIT),
        cost_estimate=pl.CostEstimate(flops=16 * rows * half, bytes_accessed=3 << 20, transcendentals=0),
        name="stage_sum",
    )(at, *parts, *after)


def middle_kernel(*refs):
    out_ref = refs[-1]
    rows = refs[0].shape[0]
    for i in range(2):
        total = refs[4 * i][...].astype(F32)
        for ref in refs[4 * i + 1 : 4 * i + 4]:
            total = total + ref[...].astype(F32)
        out_ref[i * rows : (i + 1) * rows, :] = total.astype(BF16)


def middle_sum(parts, *after):
    rows, half = parts[0].shape
    return pl.pallas_call(
        middle_kernel,
        out_shape=jax.ShapeDtypeStruct((2 * rows, half), BF16),
        in_specs=[whole_vmem()] * 8 + [anywhere()] * len(after),
        out_specs=whole_vmem(),
        cost_estimate=pl.CostEstimate(flops=8 * rows * half, bytes_accessed=2 << 20, transcendentals=0),
        name="middle_sum",
    )(*parts, *after)


def last_kernel(x_ref, out_ref):
    rows, half = x_ref.shape
    for i in range(2):
        cut = slice(i * (rows // 2), (i + 1) * (rows // 2))
        out_ref[i * half : (i + 1) * half, :] = x_ref[cut, :].astype(F32).T


def last_turn(x):
    rows, half = x.shape
    return pl.pallas_call(
        last_kernel,
        out_shape=jax.ShapeDtypeStruct((2 * half, rows // 2), F32),
        in_specs=[whole_vmem()],
        out_specs=whole_vmem(),
        cost_estimate=pl.CostEstimate(flops=rows * half, bytes_accessed=1 << 20, transcendentals=0),
        name="last_turn",
    )(x)


def encode_kernel(me_ref, q_ref, nb_ref, own_ref, left_ref, right_ref, far_ref, w_ref, out_ref, k_s, v_s, m_s):
    part = own_ref.shape[0] // 2
    me = me_ref[0]
    for step, ref in zip(STEPS, (own_ref, left_ref, right_ref, far_ref)):
        at = pl.ds(pl.multiple_of((me + step) % 4 * part, 32), part)
        k_s[at, :] = ref[:part, :]
        v_s[at, :] = ref[part:, :]
    rows, cols = q_ref.shape[0], k_s.shape[1]
    same = (
        lax.broadcasted_iota(jnp.int32, (rows, cols), 0) // BLOCK_LEN
        == lax.broadcasted_iota(jnp.int32, (rows, cols), 1) // BLOCK_LEN
    )
    for h in range(HE):
        at = slice(h * HD, (h + 1) * HD)
        s = jnp.dot(q_ref[:, at], k_s[at, :], preferred_element_type=F32) * SCALE
        s = jnp.where(same, s, NEG)
        p = jnp.exp2(s - jnp.max(s, axis=1, keepdims=True))
        p = p * (1.0 / jnp.sum(p, axis=1, keepdims=True))
        m_s[:, at] = lax.dot_general(p.astype(BF16), v_s[at, :], NT, preferred_element_type=F32).astype(BF16)
    out_ref[...] = (
        nb_ref[...].astype(F32) + jnp.dot(m_s[...], w_ref[...], preferred_element_type=F32)
    ).astype(BF16)


def encode(chunk, me, queries, neighbours, pieces, weight):
    width = neighbours.shape[1]
    rows = neighbours.shape[0] // 2
    tokens = pieces[0].shape[1]

    def whole(shape):
        return pl.BlockSpec(shape, lambda n: (0, 0))

    part = pl.BlockSpec((rows, width), lambda n: (chunk, 0))
    return pl.pallas_call(
        encode_kernel,
        grid=(1,),
        out_shape=jax.ShapeDtypeStruct((rows, width), BF16),
        in_specs=[scalars(), part, part] + [whole(pieces[0].shape)] * 4 + [whole(weight.shape)],
        out_specs=whole((rows, width)),
        scratch_shapes=[
            pltpu.VMEM((width, tokens), BF16),
            pltpu.VMEM((width, tokens), BF16),
            pltpu.VMEM((rows, width), BF16),
        ],
        compiler_params=pltpu.CompilerParams(vmem_limit_bytes=VMEM_LIMIT),
        cost_estimate=pl.CostEstimate(
            flops=2 * rows * width * (width + 2 * tokens), bytes_accessed=4 << 20, transcendentals=HE * rows * tokens
        ),
        name="encode",
    )(me, queries, neighbours, *pieces, weight)


def decode_kernel(q_ref, own_ref, left_ref, right_ref, far_ref, k_ref, v_ref, out_ref, q_s, m_s):
    heads, tokens, _ = m_s.shape
    blocks = tokens // BLOCK_LEN
    for h in range(heads):
        cut = slice(h * HD, (h + 1) * HD)
        res = lax.dot_general(q_ref[:, cut], k_ref[:, cut], NT, preferred_element_type=F32) * SCALE
        res = res.astype(BF16)
        for b in range(blocks):
            q_s[b, h * BLOCK_LEN : (h + 1) * BLOCK_LEN, :] = res[b * BLOCK_LEN : (b + 1) * BLOCK_LEN]
    for b in range(blocks):
        at = slice(b * BLOCK_LEN, (b + 1) * BLOCK_LEN)
        rows = jnp.concatenate([own_ref[at, :], left_ref[at, :], right_ref[at, :], far_ref[at, :]], axis=0)
        s = lax.dot_general(q_s[b], rows, NT, preferred_element_type=F32)
        p = jnp.exp2(s - jnp.max(s, axis=1, keepdims=True))
        p = p * (1.0 / jnp.sum(p, axis=1, keepdims=True))
        mixed = jnp.dot(p.astype(BF16), rows, preferred_element_type=F32).astype(BF16)
        for h in range(heads):
            m_s[h, at, :] = mixed[h * BLOCK_LEN : (h + 1) * BLOCK_LEN]
    for h in range(heads):
        at = slice(h * HD, (h + 1) * HD)
        out_ref[:, at] = jnp.dot(m_s[h], v_ref[:, at], preferred_element_type=F32).astype(BF16)


def decode(chunk, queries, pieces, key_weight, value_weight):
    tokens, depth = pieces[0].shape
    width = queries.shape[1]
    heads = width // HD
    blocks = tokens // BLOCK_LEN
    rows = heads * BLOCK_LEN

    def whole(shape):
        return pl.BlockSpec(shape, lambda n: (0, 0))

    return pl.pallas_call(
        decode_kernel,
        grid=(1,),
        out_shape=jax.ShapeDtypeStruct((tokens, width), BF16),
        in_specs=[pl.BlockSpec((tokens, width), lambda n: (chunk, 0))]
        + [whole(pieces[0].shape)] * 4
        + [whole(key_weight.shape)] * 2,
        out_specs=whole((tokens, width)),
        scratch_shapes=[pltpu.VMEM((blocks, rows, depth), BF16), pltpu.VMEM((heads, tokens, depth), BF16)],
        compiler_params=pltpu.CompilerParams(vmem_limit_bytes=VMEM_LIMIT),
        cost_estimate=pl.CostEstimate(
            flops=4 * tokens * depth * (heads * 256 + width), bytes_accessed=7 << 20, transcendentals=blocks * rows * 256
        ),
        name="decode",
    )(queries, *pieces, key_weight, value_weight)


def per_device(
    hidden,
    neighbours,
    block_map,
    enc_key_weight,
    enc_value_weight,
    enc_query_weight,
    enc_out_weight,
    query_weight,
    key_weight,
    value_weight,
    out_weight,
    cotangent,
):
    me = lax.axis_index("tp")
    me_vec = me.reshape(1).astype(jnp.int32)
    core = lax.axis_index("core")
    yg = lax.axis_index("grp") * 2 + lax.axis_index("yhi")
    spot = jnp.stack([lax.axis_index("z"), yg, core, 1 - core]).astype(jnp.int32)
    self_index = lax.axis_index(YZC)
    devices = 32
    local_count, positions, depth = neighbours.shape
    tok_rows, feat = hidden.shape
    chunks = 2
    chunk = tok_rows // chunks

    flat_map = block_map.reshape(devices, local_count)
    owners = flat_map // local_count
    places = flat_map % local_count
    order = jnp.arange(local_count, dtype=jnp.int32)
    send_place = jnp.sum(jnp.where(owners == self_index, places, 0), axis=1)
    my_owners = lax.dynamic_index_in_dim(owners, self_index, 0, keepdims=False)
    everyone = jnp.arange(devices, dtype=jnp.int32)
    back_slot = jnp.sum(jnp.where(my_owners[None, :] == everyone[:, None], order[None, :], 0), axis=1)
    wanted = self_index * local_count + order
    asker = jnp.sum(
        jnp.where(
            flat_map.reshape(1, -1) == wanted[:, None],
            (jnp.arange(devices * local_count, dtype=jnp.int32) // local_count)[None, :],
            0,
        ),
        axis=1,
    )

    ways = (1, -1)
    sent = pick([neighbours], send_place)
    left = lax.ppermute(hidden, "tp", ring(1))
    right = lax.ppermute(hidden, "tp", ring(-1))
    begun = query(me_vec, (0,), (hidden,), query_weight, None, F32)
    fars = [
        lax.ppermute(rows_of(left, 0, sent, begun), "tp", ring(1)),
        lax.ppermute(rows_of(right, 1), "tp", ring(-1)),
    ]
    nearer = query(me_vec, (3, 1), (left, right), query_weight, begun, F32)

    came = lax.all_to_all(sent, YZC, split_axis=0, concat_axis=0, tiled=True)
    mine, enc_queries = take_queries(came, my_owners, enc_query_weight)

    kv_pieces = []
    for i in range(chunks):
        after = () if i else (nearer,)
        pairs = key_value(i, me_vec, (hidden, left, right), fars[i], enc_key_weight.T, enc_value_weight.T, *after)
        kv_pieces.append(gather_direct(pairs))
    queries = query(me_vec, (2,), fars, query_weight, nearer, BF16)

    out_all = lax.all_gather(out_weight, YZC, axis=0)

    encoded_parts = []
    encoded_pieces = []
    for i in range(chunks):
        part = encode(i, me_vec, enc_queries, mine, kv_pieces[i], enc_out_weight)
        encoded_parts.append(part.reshape(local_count // chunks, positions, depth))
        encoded_pieces.append(gather_ring(part, ways[i]))

    back = lax.all_to_all(pick(encoded_parts, back_slot), YZC, split_axis=0, concat_axis=0, tiled=True)
    encoded = pick([back], asker)

    own = [decode(i, queries, encoded_pieces[i], key_weight, value_weight) for i in range(chunks)]
    attended = gather_ring(own[0], ways[0]) + gather_ring(own[1], ways[1])
    term = project(*own, out_all)

    others, sent_sums = [], []
    for half in range(2):
        sums = product_send(half, spot, attended, cotangent, *(() if half else (encoded, term)))
        sent_sums.append(sums)
        others.append(lax.ppermute(sums, "core", [(0, 1), (1, 0)]))
    by_z = product_keep(True, 0, spot, attended, cotangent, others[0])
    by_z = [by_z[0]] + [lax.ppermute(by_z[d], "z", ring(d)) for d in (1, 3, 2)]
    by_y = product_keep(False, 1, spot, attended, cotangent, others[1])
    by_y = [by_y[0]] + [lax.ppermute(by_y[d], ("grp", "yhi"), y_pairs(d // 2, d % 2)) for d in (1, 2, 3)]
    projected = lax.psum_scatter(held(term, sent_sums[0]), "tp", scatter_dimension=1, tiled=True)
    to_y = stage_sum(True, spot, by_z)
    to_y = [to_y[0]] + [lax.ppermute(to_y[d], ("grp", "yhi"), y_pairs(d // 2, d % 2)) for d in (1, 2, 3)]
    to_z = stage_sum(False, spot, by_y)
    to_z = [to_z[0]] + [lax.ppermute(to_z[d], "z", ring(d)) for d in (1, 3, 2)]
    layer_output = (hidden.astype(F32) + projected.astype(F32)).astype(BF16)
    grad = last_turn(lax.ppermute(middle_sum(to_y + to_z, layer_output), AXES, owner_pairs()))
    return (layer_output, encoded, grad)


def solution(mesh):
    fine = Mesh(mesh.devices.reshape(2, 4, 2, 2, 4), AXES)
    placed = (
        P(YZC, "tp"),
        P(YZC, "tp", None),
        P(),
        P(None, "tp"),
        P(None, "tp"),
        P(),
        P(),
        P(None, "tp"),
        P(None, "tp"),
        P(None, "tp"),
        P("tp", YZC),
        P(YZC, "tp"),
    )
    return jax.shard_map(
        per_device,
        mesh=fine,
        in_specs=placed,
        out_specs=(P(YZC, "tp"), P(YZC, "tp", None), P("tp", YZC)),
        check_vma=False,
    )
```
